32 devices in a mesh: row: 4 (over z), col: 8 (over y, x, core).
Axes of the slice: x: 2, y: 2, z: 4, core: 2. Of those that a mesh axis runs over, the one named last changes fastest.
Arguments:
- nodes: bfloat16 [16384, 512], P(('row', 'col')), may hold values from -6 to 6
- cotangent: bfloat16 [16384, 512], P(('row', 'col')), may hold values from -6 to 6
- edge_source: int32 [65536], P(('row', 'col')), may hold values from 0 to 639
- edge_target: int32 [65536], P(('row', 'col')), may hold values from 0 to 511
- halo_lists: int32 [32, 4, 32], P(('row', 'col')), may hold values from 0 to 511
- pool_owner: int32 [16384], P(('row', 'col')), may hold values from 0 to 31, as said below
- pool_table: int32 [32, 1024], P(('row', 'col')), may hold values from -1 to 127, as said below
- source_weight: bfloat16 [512, 512], replicated, may hold values from -0.25 to 0.25
- target_weight: bfloat16 [512, 512], replicated, may hold values from -0.25 to 0.25
- edge_weight: bfloat16 [512, 512], replicated, may hold values from -0.25 to 0.25
- inner_weight: bfloat16 [1024, 512], replicated, may hold values from -0.1875 to 0.1875
- outer_weight: bfloat16 [512, 512], replicated, may hold values from -0.25 to 0.25
- coarse_weight: bfloat16 [512, 512], replicated, may hold values from -0.5 to 0.5
Outputs:
- updated: bfloat16 [16384, 512], P(('row', 'col'))
- node_gradient: float32 [16384, 512], P(('row', 'col'))
- source_gradient: float32 [512, 512], replicated
- target_gradient: float32 [512, 512], replicated
- edge_gradient: float32 [512, 512], replicated
- inner_gradient: float32 [1024, 512], replicated
- outer_gradient: float32 [512, 512], replicated
- coarse_gradient: float32 [512, 512], replicated
The draws below stay inside these ranges and needn't reach their ends.
Inputs may be any that keep to these rules, and one draw needn't show every extreme that they name: `edge_source`: rows below 512 are the partition's own nodes; row 512 + k * 32 + j is row j of halo block k. `pool_owner`: at most 32 nodes of one partition name the same owner; one owner is named by exactly 32 nodes of every partition. `pool_table`: entry [o, q * 32 + k] is the coarse row of owner o for the node of rank k among the nodes of partition q that name o, and -1 where q names o fewer than k + 1 times.
All inputs are finite; a program needn't handle non-finite values.
Results may differ from the reference program's by a relative error of at most 0.014.
Values may be sent and summed in bfloat16 or wider, within the bound.
A program may use at most 128 MiB of HBM per device.

```python
import math
import jax
import jax.numpy as jnp
from jax import lax

W = 512
NODE_DEV = 512
EDGE_DEV = 2048
HALO = 32
COARSE_DEV = 128
CAP = 32
NODES = 16384
EDGES = 65536
N_ROW = 4
N_COL = 8
DEVICES = 32


def pooling_plan(key):
    busy_key = jax.random.fold_in(key, 11)
    score_key = jax.random.fold_in(key, 12)
    order_key = jax.random.fold_in(key, 13)
    row_key = jax.random.fold_in(key, 14)
    slots = DEVICES * CAP
    busy = jax.random.randint(busy_key, (), 0, DEVICES)
    places = jnp.arange(slots, dtype=jnp.int32)
    scores = jax.random.randint(score_key, (DEVICES, slots), 0, 32768) * slots + places[None, :]
    bucket = places // CAP
    scores = jnp.where((bucket == busy)[None, :], 2 ** 30 + places[None, :], scores)
    chosen = lax.top_k(scores, NODE_DEV)[1]
    chosen_owner = (chosen // CAP).astype(jnp.int32)
    counts = jnp.sum((chosen_owner[:, :, None] == jnp.arange(DEVICES, dtype=jnp.int32)[None, None, :]).astype(jnp.int32), axis=1)
    shuffle = jax.random.randint(order_key, (DEVICES, NODE_DEV), 0, 65536) * NODE_DEV + jnp.arange(NODE_DEV, dtype=jnp.int32)[None, :]
    order = jnp.argsort(shuffle, axis=1)
    owner = jnp.take_along_axis(chosen_owner, order, axis=1)
    live = jnp.arange(CAP, dtype=jnp.int32)[None, None, :] < counts[:, :, None]
    rows = jax.random.randint(row_key, (DEVICES, DEVICES, CAP), 0, COARSE_DEV)
    table = jnp.where(jnp.transpose(live, (1, 0, 2)), rows, -1).reshape(DEVICES, slots)
    return (owner.reshape(DEVICES * NODE_DEV).astype(jnp.int32), table.astype(jnp.int32))


def draw_pool_owner(key, part):
    return pooling_plan(key)[0]


def draw_pool_table(key, part):
    return pooling_plan(key)[1]


def set_ends(values, own_key, smallest, high):
    longest = values.shape.index(max(values.shape))
    spots = []
    for shift in (0, 1):
        where = [jax.random.randint(jax.random.fold_in(own_key, axis), (), 0, length) for axis, length in enumerate(values.shape)]
        where[longest] = (where[longest] + shift) % values.shape[longest]
        spots.append(tuple(where))
    return values.at[spots[0]].set(smallest).at[spots[1]].set(high)


def block_levels(key, shape, split, least, high):
    factor_of, own = 1.0, jax.random.fold_in(key, 6)
    for axis_at, parts in split:
        heights = jnp.exp(jax.random.uniform(jax.random.fold_in(own, axis_at), (parts,), jnp.float32, least / len(split), high / len(split)))
        factor_of = factor_of * jnp.repeat(heights, shape[axis_at] // parts).reshape([-1 if axis == axis_at else 1 for axis in range(len(shape))])
    return factor_of


def centred(key, extent, deviation, bound, cuts=(), held_as=jnp.bfloat16):
    drawn = jax.random.normal(key, extent, jnp.float32) * deviation
    if len(cuts) > 0:
        drawn = block_levels(key, extent, cuts, -0.22, 0.18) * drawn
    return jnp.clip(drawn, min=-bound, max=bound).astype(held_as)


def setup_inputs(seed: int = 0) -> dict:
    key_of = jax.random.split(jax.random.key(seed), 14)
    return {
        "nodes": centred(key_of[0], (NODES, W), 1.0, 6.0, ((0, 32),)),
        "cotangent": centred(key_of[1], (NODES, W), 1.0, 6.0, ((0, 32),)),
        "edge_source": set_ends(jax.random.randint(key_of[2], (EDGES,), 0, NODE_DEV + 4 * HALO), jax.random.fold_in(key_of[2], 1), 0, (NODE_DEV + 4 * HALO) - 1).astype(jnp.int32),
        "edge_target": set_ends(jax.random.randint(key_of[3], (EDGES,), 0, NODE_DEV), jax.random.fold_in(key_of[3], 1), 0, NODE_DEV - 1).astype(jnp.int32),
        "halo_lists": set_ends(jax.random.randint(key_of[4], (DEVICES, 4, HALO), 0, NODE_DEV), jax.random.fold_in(key_of[4], 1), 0, NODE_DEV - 1).astype(jnp.int32),
        "pool_owner": draw_pool_owner(jax.random.fold_in(key_of[13], 71), 0),
        "pool_table": draw_pool_table(jax.random.fold_in(key_of[13], 71), 0),
        "source_weight": centred(key_of[7], (W, W), W ** -0.5, 0.25),
        "target_weight": centred(key_of[8], (W, W), W ** -0.5, 0.25),
        "edge_weight": centred(key_of[9], (W, W), W ** -0.5, 0.25),
        "inner_weight": centred(key_of[10], (2 * W, W), (2 * W) ** -0.5, 0.1875),
        "outer_weight": centred(key_of[11], (W, W), W ** -0.5, 0.25),
        "coarse_weight": centred(key_of[12], (W, W), (W // 4) ** -0.5, 0.5),
    }


def product(first, second):
    return jnp.dot(first, second, preferred_element_type=jnp.float32)

def left_product(first, second):
    return lax.dot_general(first, second, (((0,), (0,)), ((), ())), preferred_element_type=jnp.float32)

def right_product(first, second):
    return lax.dot_general(first, second, (((1,), (1,)), ((), ())), preferred_element_type=jnp.float32)

def silu_slope(value):
    sigma = jax.nn.sigmoid(value)
    return sigma * (1.0 + value * (1.0 - sigma))

def shift_grid(blocks, axis, offset):
    length = blocks.shape[axis]
    rolled = jnp.roll(blocks, offset, axis=axis)
    anchor = jnp.arange(length) - offset
    keep = (anchor >= 0) & (anchor < length)
    shape = [1] * blocks.ndim
    shape[axis] = length
    return jnp.where(keep.reshape(shape), rolled, jnp.zeros_like(rolled))

def pick_rows(rows, lists):
    return jnp.take(rows, lists.reshape(-1), axis=0)

def add_returns(grads, lists, values):
    return grads.at[lists.reshape(-1)].add(values.astype(jnp.float32))

def local_forward(nodes_part, halo_part, source_part, target_part, weights):
    source_weight, target_weight, edge_weight, inner_weight, outer_weight = weights
    extended = jnp.concatenate([nodes_part, halo_part], axis=0)
    source_side = product(extended, source_weight)
    target_side = product(nodes_part, target_weight)
    edge_linear = jnp.take(source_side, source_part, axis=0) + jnp.take(target_side, target_part, axis=0)
    edge_hidden = jax.nn.silu(edge_linear).astype(jnp.bfloat16)
    message_linear = product(edge_hidden, edge_weight)
    aggregate = jax.ops.segment_sum(jax.nn.silu(message_linear), target_part, NODE_DEV).astype(jnp.bfloat16)
    joined = jnp.concatenate([nodes_part, aggregate], axis=1)
    node_linear = product(joined, inner_weight)
    node_hidden = jax.nn.silu(node_linear).astype(jnp.bfloat16)
    refined = (nodes_part.astype(jnp.float32) + product(node_hidden, outer_weight)).astype(jnp.bfloat16)
    return (extended, edge_linear, edge_hidden, message_linear, joined, node_linear, node_hidden, refined)

def reference(nodes, cotangent, edge_source, edge_target, halo_lists, pool_owner, pool_table, source_weight, target_weight, edge_weight, inner_weight, outer_weight, coarse_weight):
    weights = (source_weight, target_weight, edge_weight, inner_weight, outer_weight)
    node_parts = nodes.reshape(DEVICES, NODE_DEV, W)
    sent = jax.vmap(pick_rows)(node_parts, halo_lists).reshape(N_ROW, N_COL, 4, HALO, W)
    blocks = [shift_grid(sent[:, :, 0], 0, 1), shift_grid(sent[:, :, 1], 0, -1), shift_grid(sent[:, :, 2], 1, 1), shift_grid(sent[:, :, 3], 1, -1)]
    halo_parts = jnp.stack(blocks, axis=2).reshape(DEVICES, 4 * HALO, W)
    source_parts = edge_source.reshape(DEVICES, EDGE_DEV)
    target_parts = edge_target.reshape(DEVICES, EDGE_DEV)

    def forward_part(inputs):
        return local_forward(inputs[0], inputs[1], inputs[2], inputs[3], weights)[-1]
    refined = lax.map(forward_part, (node_parts, halo_parts, source_parts, target_parts)).reshape(NODES, W)
    owners = pool_owner.reshape(DEVICES, NODE_DEV)
    owner_hot = (owners[:, :, None] == jnp.arange(DEVICES, dtype=jnp.int32)[None, None, :]).astype(jnp.int32)
    rank = lax.optimization_barrier(jnp.sum((jnp.cumsum(owner_hot, axis=1) - 1) * owner_hot, axis=2)).astype(jnp.int32)
    column = jnp.arange(DEVICES, dtype=jnp.int32)[:, None] * CAP + rank
    parent = (owners * COARSE_DEV + pool_table[owners, column]).reshape(NODES).astype(jnp.int32)
    coarse_total = DEVICES * COARSE_DEV
    count = jnp.maximum(jax.ops.segment_sum(jnp.ones((NODES,), jnp.float32), parent, coarse_total), 1.0)[:, None]
    coarse = (jax.ops.segment_sum(refined.astype(jnp.float32), parent, coarse_total) / count).astype(jnp.bfloat16)
    coarse_linear = product(coarse, coarse_weight)
    coarse_update = jax.nn.silu(coarse_linear).astype(jnp.bfloat16)
    updated = (refined.astype(jnp.float32) + jnp.take(coarse_update, parent, axis=0).astype(jnp.float32)).astype(jnp.bfloat16)
    grad_coarse = (jax.ops.segment_sum(cotangent.astype(jnp.float32), parent, coarse_total) * silu_slope(coarse_linear)).astype(jnp.bfloat16)
    coarse_gradient = left_product(coarse, grad_coarse)
    coarse_share = (right_product(grad_coarse, coarse_weight) / count).astype(jnp.bfloat16)
    grad_refined = cotangent.astype(jnp.float32) + jnp.take(coarse_share, parent, axis=0).astype(jnp.float32)

    def backward_part(totals, inputs):
        nodes_part, halo_part, source_part, target_part, refined_grad = inputs
        extended, edge_linear, edge_hidden, message_linear, joined, node_linear, node_hidden, unused_rows = local_forward(nodes_part, halo_part, source_part, target_part, weights)
        refined_low = refined_grad.astype(jnp.bfloat16)
        outer_part = left_product(node_hidden, refined_low)
        grad_hidden = (right_product(refined_low, outer_weight) * silu_slope(node_linear)).astype(jnp.bfloat16)
        inner_part = left_product(joined, grad_hidden)
        grad_joined = right_product(grad_hidden, inner_weight)
        grad_aggregate = grad_joined[:, W:].astype(jnp.bfloat16)
        grad_message = (jnp.take(grad_aggregate, target_part, axis=0) * silu_slope(message_linear)).astype(jnp.bfloat16)
        edge_part = left_product(edge_hidden, grad_message)
        grad_edges = right_product(grad_message, edge_weight) * silu_slope(edge_linear)
        grad_sources = jax.ops.segment_sum(grad_edges, source_part, NODE_DEV + 4 * HALO).astype(jnp.bfloat16)
        grad_targets = jax.ops.segment_sum(grad_edges, target_part, NODE_DEV).astype(jnp.bfloat16)
        source_part_grad = left_product(extended, grad_sources)
        target_part_grad = left_product(nodes_part, grad_targets)
        grad_extended = right_product(grad_sources, source_weight)
        local_grad = refined_grad + grad_joined[:, :W] + right_product(grad_targets, target_weight) + grad_extended[:NODE_DEV]
        halo_grad = grad_extended[NODE_DEV:].astype(jnp.bfloat16)
        totals = (totals[0] + source_part_grad, totals[1] + target_part_grad, totals[2] + edge_part, totals[3] + inner_part, totals[4] + outer_part)
        return (totals, (local_grad, halo_grad))
    square = jnp.zeros((W, W), jnp.float32)
    start = (square, square, square, jnp.zeros((2 * W, W), jnp.float32), square)
    totals, outputs = lax.scan(backward_part, start, (node_parts, halo_parts, source_parts, target_parts, grad_refined.reshape(DEVICES, NODE_DEV, W)))
    local_grads, halo_grads = outputs
    halo_grid = halo_grads.reshape(N_ROW, N_COL, 4, HALO, W)
    back = [shift_grid(halo_grid[:, :, 0], 0, -1), shift_grid(halo_grid[:, :, 1], 0, 1), shift_grid(halo_grid[:, :, 2], 1, -1), shift_grid(halo_grid[:, :, 3], 1, 1)]
    returned = jnp.stack(back, axis=2).reshape(DEVICES, 4 * HALO, W)
    node_gradient = jax.vmap(add_returns)(local_grads, halo_lists, returned).reshape(NODES, W)
    scale = 1.0 / math.sqrt(NODES)
    return (updated, node_gradient, totals[0] * scale, totals[1] * scale, totals[2] * scale, totals[3] * scale, totals[4] * scale, coarse_gradient * scale)
```

```python
import math

import jax
import jax.numpy as jnp
from jax import lax
from jax.sharding import PartitionSpec as P


def passed_along(value, axis, steps):
    count = lax.axis_size(axis)
    initial, last = (max(0, -steps), min(count, count - steps))
    return lax.ppermute(value, axis, [(source, source + steps) for source in range(initial, last)])


def product(first, second):
    return jnp.dot(first, second, preferred_element_type=jnp.float32)


def left_product(first, second):
    return lax.dot_general(
        first, second, (((0,), (0,)), ((), ())), preferred_element_type=jnp.float32
    )


def right_product(first, second):
    return lax.dot_general(
        first, second, (((1,), (1,)), ((), ())), preferred_element_type=jnp.float32
    )


def silu_slope(value):
    sigma = jax.nn.sigmoid(value)
    return sigma * (1.0 + value * (1.0 - sigma))


def one_hot(index, rows):
    return (index[:, None] == jnp.arange(rows, dtype=jnp.int32)[None, :]).astype(jnp.bfloat16)


def low(value):
    return value.astype(jnp.bfloat16)


def trade_halo(blocks, flip):
    moved = []
    for number, offset in enumerate((1, -1)):
        moved.append(passed_along(blocks[number], "row", offset * flip))
    for number, offset in enumerate((1, -1)):
        moved.append(passed_along(blocks[2 + number], "col", offset * flip))
    return moved


def trade_slots(buffer):
    return lax.all_to_all(buffer, ("row", "col"), split_axis=0, concat_axis=0, tiled=True)


def local(
    nodes,
    cotangent,
    edge_source,
    edge_target,
    halo_lists,
    pool_owner,
    pool_table,
    source_weight,
    target_weight,
    edge_weight,
    inner_weight,
    outer_weight,
    coarse_weight,
):
    devices = lax.axis_size("row") * lax.axis_size("col")
    count_rows, width = nodes.shape
    lists = halo_lists[0]
    halo_rows = lists.shape[1]
    table = pool_table[0]
    capacity = table.shape[0] // devices
    coarse_rows = count_rows // 4
    scale = 1.0 / math.sqrt(count_rows * devices)
    all_lists = lists.reshape(-1)
    owner_hot = one_hot(pool_owner, devices)
    positions = jnp.arange(count_rows, dtype=jnp.int32)
    lower = (positions[:, None] > positions[None, :]).astype(jnp.bfloat16)
    rank = jnp.sum(product(lower, owner_hot) * owner_hot, axis=1).astype(jnp.int32)
    slot = pool_owner * capacity + rank
    slot_hot = one_hot(slot, devices * capacity)
    member = (jnp.arange(coarse_rows, dtype=jnp.int32)[:, None] == table[None, :]).astype(
        jnp.bfloat16
    )
    count = jnp.maximum(jnp.sum(member, axis=1, dtype=jnp.float32), 1.0)[:, None]

    def toward_owners(values):
        return product(member, trade_slots(low(left_product(slot_hot, values))))

    def toward_sources(values):
        return product(slot_hot, trade_slots(low(left_product(member, values))))

    list_hot = one_hot(all_lists, count_rows)
    picked = low(product(list_hot, nodes)).reshape(4, halo_rows, width)
    received = trade_halo([picked[number] for number in range(4)], 1)
    pooled_cotangent = toward_owners(cotangent)
    extended = jnp.concatenate([nodes] + received, axis=0)
    source_hot = one_hot(edge_source, extended.shape[0])
    target_hot = one_hot(edge_target, count_rows)
    source_side = low(product(extended, source_weight))
    target_side = low(product(nodes, target_weight))
    edge_linear = product(source_hot, source_side) + product(target_hot, target_side)
    edge_hidden = low(jax.nn.silu(edge_linear))
    message_linear = product(edge_hidden, edge_weight)
    aggregate = low(left_product(target_hot, low(jax.nn.silu(message_linear))))
    joined = jnp.concatenate([nodes, aggregate], axis=1)
    node_linear = product(joined, inner_weight)
    node_hidden = low(jax.nn.silu(node_linear))
    refined = low(nodes.astype(jnp.float32) + product(node_hidden, outer_weight))
    coarse = low(toward_owners(refined) / count)
    coarse_linear = product(coarse, coarse_weight)
    coarse_update = low(jax.nn.silu(coarse_linear))
    grad_coarse = low(pooled_cotangent * silu_slope(coarse_linear))
    coarse_share = low(right_product(grad_coarse, coarse_weight) / count)
    share_rows = toward_sources(coarse_share)
    updated = low(refined.astype(jnp.float32) + toward_sources(coarse_update))
    coarse_gradient = left_product(coarse, grad_coarse)
    grad_refined = cotangent.astype(jnp.float32) + share_rows
    refined_low = low(grad_refined)
    outer_gradient = left_product(node_hidden, refined_low)
    grad_hidden = low(right_product(refined_low, outer_weight) * silu_slope(node_linear))
    inner_gradient = left_product(joined, grad_hidden)
    grad_joined = right_product(grad_hidden, inner_weight)
    grad_aggregate = low(grad_joined[:, width:])
    grad_message = low(product(target_hot, grad_aggregate) * silu_slope(message_linear))
    edge_gradient = left_product(edge_hidden, grad_message)
    grad_edges = low(right_product(grad_message, edge_weight) * silu_slope(edge_linear))
    grad_sources = low(left_product(source_hot, grad_edges))
    grad_targets = low(left_product(target_hot, grad_edges))
    source_gradient = left_product(extended, grad_sources)
    target_gradient = left_product(nodes, grad_targets)
    gradients = (
        source_gradient,
        target_gradient,
        edge_gradient,
        inner_gradient,
        outer_gradient,
        coarse_gradient,
    )
    sizes = [gradient.shape[0] for gradient in gradients]
    stacked = jnp.concatenate([low(gradient * scale) for gradient in gradients], axis=0)
    share = lax.psum_scatter(stacked, ("row", "col"), scatter_dimension=0, tiled=True)
    summed = lax.all_gather(share, ("row", "col"), axis=0, tiled=True).astype(jnp.float32)
    starts = [sum(sizes[:number]) for number in range(len(sizes))]
    totals = [
        lax.slice_in_dim(summed, start, start + size, axis=0)
        for start, size in zip(starts, sizes)
    ]
    grad_extended = right_product(grad_sources, source_weight)
    back_blocks = low(grad_extended[count_rows:]).reshape(4, halo_rows, width)
    returned = trade_halo([back_blocks[number] for number in range(4)], -1)
    node_gradient = (
        grad_refined
        + grad_joined[:, :width]
        + right_product(grad_targets, target_weight)
        + grad_extended[:count_rows]
        + left_product(list_hot, jnp.concatenate(returned, axis=0))
    )
    return (updated, node_gradient, *totals)


def solution(mesh):
    in_specs = (
        P(("row", "col"), None),
        P(("row", "col"), None),
        P(("row", "col")),
        P(("row", "col")),
        P(("row", "col"), None, None),
        P(("row", "col")),
        P(("row", "col"), None),
        P(),
        P(),
        P(),
        P(),
        P(),
        P(),
    )
    out_specs = (P(("row", "col"), None), P(("row", "col"), None), P(), P(), P(), P(), P(), P())
    return jax.shard_map(local, mesh=mesh, in_specs=in_specs, out_specs=out_specs, check_vma=False)
```

```python
import functools
import math

import jax
import jax.numpy as jnp
from jax import lax
from jax.experimental import pallas as pl
from jax.experimental.pallas import tpu as pltpu
from jax.sharding import PartitionSpec as P


def passed_along(value, axis, steps):
    count = lax.axis_size(axis)
    initial, last = (max(0, -steps), min(count, count - steps))
    return lax.ppermute(value, axis, [(source, source + steps) for source in range(initial, last)])


def product(first, second):
    return jnp.dot(first, second, preferred_element_type=jnp.float32)


def left_product(first, second):
    return lax.dot_general(
        first, second, (((0,), (0,)), ((), ())), preferred_element_type=jnp.float32
    )


def right_product(first, second):
    return lax.dot_general(
        first, second, (((1,), (1,)), ((), ())), preferred_element_type=jnp.float32
    )


def silu_slope(value):
    sigma = jax.nn.sigmoid(value)
    return sigma * (1.0 + value * (1.0 - sigma))


def one_hot(index, rows):
    return (index[:, None] == jnp.arange(rows, dtype=jnp.int32)[None, :]).astype(jnp.bfloat16)


def low(value):
    return value.astype(jnp.bfloat16)


def trade_halo(blocks, flip):
    moved = []
    for number, offset in enumerate((1, -1)):
        moved.append(passed_along(blocks[number], "row", offset * flip))
    for number, offset in enumerate((1, -1)):
        moved.append(passed_along(blocks[2 + number], "col", offset * flip))
    return moved


def trade_slots(buffer):
    return lax.all_to_all(buffer, ("row", "col"), split_axis=0, concat_axis=0, tiled=True)


class Summation:
    def __init__(self, rows, cols, own, land, out, send, recv):
        self.rows, self.cols, self.devices = rows, cols, rows * cols
        self.bits = cols.bit_length() - 1
        self.own, self.land, self.out, self.send, self.recv = own, land, out, send, recv
        self.row, self.col = lax.axis_index("row"), lax.axis_index("col")
        self.orders = []
        rest = list(range(1, self.bits))
        for half in range(2):
            self.orders.append([0] + (rest if half == 0 else rest[::-1]))
        self.bases = []
        for order in self.orders:
            base, bases = jnp.int32(0), [jnp.int32(0)]
            for stage, bit in enumerate(order):
                base = base + self.digit(bit) * (self.devices >> (stage + 1))
                bases.append(base)
            self.bases.append(bases)
        self.steps = 2 * (self.bits + 1)

    @staticmethod
    def semaphores(rows, cols):
        return 2 * (cols.bit_length() - 1 + rows - 1)

    def digit(self, bit):
        return lax.rem(lax.div(self.col, jnp.int32(1 << bit)), jnp.int32(2))

    def across(self, bit):
        return self.col + (1 - 2 * self.digit(bit)) * (1 << bit)

    def along(self, step):
        return lax.rem(self.row + step, jnp.int32(self.rows))

    def copy(self, half, number, source, target, row, col):
        return pltpu.make_async_remote_copy(
            src_ref=source,
            dst_ref=target,
            send_sem=self.send.at[half, number],
            recv_sem=self.recv.at[half, number],
            device_id=(row, col),
            device_id_type=pl.DeviceIdType.MESH,
        )

    def copies(self, half, step):
        bits, bases = self.bits, self.bases[half]
        found = []
        if step < bits:
            size = self.devices >> (step + 1)
            bit = self.orders[half][step]
            start = bases[step] + (1 - self.digit(bit)) * size
            slot = self.devices - (self.devices >> step)
            found.append(
                self.copy(
                    half,
                    step,
                    self.own.at[half, pl.ds(start, size)],
                    self.land.at[half, pl.ds(slot, size)],
                    self.row,
                    self.across(bit),
                )
            )
        elif step == bits:
            for ahead in range(1, self.rows):
                peer = self.along(ahead)
                found.append(
                    self.copy(
                        half,
                        bits + ahead - 1,
                        self.own.at[half, pl.ds(bases[bits] + peer, 1)],
                        self.land.at[half, pl.ds(self.devices - self.rows + ahead - 1, 1)],
                        peer,
                        self.col,
                    )
                )
        elif step == bits + 1:
            for ahead in range(1, self.rows):
                mine = self.out.at[half, pl.ds(bases[bits] + self.row, 1)]
                found.append(
                    self.copy(
                        half,
                        2 * bits + self.rows - 1 + ahead - 1,
                        mine,
                        mine,
                        self.along(ahead),
                        self.col,
                    )
                )
        else:
            stage = 2 * bits + 1 - step
            size = self.devices >> (stage + 1)
            mine = self.out.at[half, pl.ds(bases[stage + 1], size)]
            found.append(
                self.copy(
                    half,
                    bits + self.rows - 1 + stage,
                    mine,
                    mine,
                    self.row,
                    self.across(self.orders[half][stage]),
                )
            )
        return found

    def start(self, half, step):
        for copy in self.copies(half, step):
            copy.start()

    def finish(self, half, step):
        for copy in self.copies(half, step):
            copy.wait()
        bits, bases = self.bits, self.bases[half]
        if step < bits:
            size = self.devices >> (step + 1)
            slot = self.devices - (self.devices >> step)

            def add(index, carry):
                here = bases[step + 1] + index
                self.own[half, here] = self.own[half, here] + self.land[half, slot + index]
                return carry

            lax.fori_loop(0, size, add, 0)
        elif step == bits:
            total = self.own[half, bases[bits] + self.row].astype(jnp.float32)
            for ahead in range(1, self.rows):
                total += self.land[half, self.devices - self.rows + ahead - 1].astype(jnp.float32)
            self.out[half, bases[bits] + self.row] = total.astype(jnp.bfloat16)

    def begin(self):
        for half in range(2):
            self.start(half, 0)

    def advance(self, step):
        for half in range(2):
            self.finish(half, step)
            if step + 1 < self.steps:
                self.start(half, step + 1)

    def greet(self):
        barrier = pltpu.get_barrier_semaphore()
        peers = [(self.row, self.across(bit)) for bit in range(self.bits)]
        peers += [(self.along(ahead), self.col) for ahead in range(1, self.rows)]
        for peer in peers:
            pl.semaphore_signal(
                barrier, inc=1, device_id=peer, device_id_type=pl.DeviceIdType.MESH
            )
        pl.semaphore_wait(barrier, len(peers))


def summation_kernel(rows, cols, terms, out, own, land, send, recv, local_sem):
    summation = Summation(rows, cols, own, land, out, send, recv)
    load = pltpu.make_async_copy(terms, own, local_sem)
    load.start()
    summation.greet()
    load.wait()
    summation.begin()
    for step in range(summation.steps):
        summation.advance(step)


def summed_over_devices(stacked):
    rows, cols = lax.axis_size("row"), lax.axis_size("col")
    devices = rows * cols
    height, width = stacked.shape
    chunk = -(-height // (16 * devices)) * 16
    padded = jnp.pad(stacked, ((0, chunk * devices - height), (0, 0)))
    halves = padded.reshape(devices, chunk, 2, width // 2).transpose(2, 0, 1, 3)
    shape = halves.shape
    count = Summation.semaphores(rows, cols)
    summed = pl.pallas_call(
        functools.partial(summation_kernel, rows, cols),
        out_shape=jax.ShapeDtypeStruct(shape, jnp.bfloat16),
        in_specs=[pl.BlockSpec(memory_space=pl.ANY)],
        out_specs=pl.BlockSpec(memory_space=pltpu.VMEM),
        scratch_shapes=[
            pltpu.VMEM(shape, jnp.bfloat16),
            pltpu.VMEM(shape, jnp.bfloat16),
            pltpu.SemaphoreType.DMA((2, count)),
            pltpu.SemaphoreType.DMA((2, count)),
            pltpu.SemaphoreType.DMA,
        ],
        compiler_params=pltpu.CompilerParams(
            collective_id=1, has_side_effects=True, vmem_limit_bytes=48 << 20
        ),
    )(halves)
    return summed.transpose(1, 2, 0, 3).reshape(devices * chunk, width)[:height]


def local(
    nodes,
    cotangent,
    edge_source,
    edge_target,
    halo_lists,
    pool_owner,
    pool_table,
    source_weight,
    target_weight,
    edge_weight,
    inner_weight,
    outer_weight,
    coarse_weight,
):
    devices = lax.axis_size("row") * lax.axis_size("col")
    count_rows, width = nodes.shape
    lists = halo_lists[0]
    halo_rows = lists.shape[1]
    table = pool_table[0]
    capacity = table.shape[0] // devices
    coarse_rows = count_rows // 4
    scale = 1.0 / math.sqrt(count_rows * devices)
    all_lists = lists.reshape(-1)
    owner_hot = one_hot(pool_owner, devices)
    positions = jnp.arange(count_rows, dtype=jnp.int32)
    lower = (positions[:, None] > positions[None, :]).astype(jnp.bfloat16)
    rank = jnp.sum(product(lower, owner_hot) * owner_hot, axis=1).astype(jnp.int32)
    slot = pool_owner * capacity + rank
    slot_hot = one_hot(slot, devices * capacity)
    member = (jnp.arange(coarse_rows, dtype=jnp.int32)[:, None] == table[None, :]).astype(
        jnp.bfloat16
    )
    count = jnp.maximum(jnp.sum(member, axis=1, dtype=jnp.float32), 1.0)[:, None]

    def toward_owners(values):
        return product(member, trade_slots(low(left_product(slot_hot, values))))

    def toward_sources(values):
        return product(slot_hot, trade_slots(low(left_product(member, values))))

    list_hot = one_hot(all_lists, count_rows)
    picked = low(product(list_hot, nodes)).reshape(4, halo_rows, width)
    received = trade_halo([picked[number] for number in range(4)], 1)
    pooled_cotangent = toward_owners(cotangent)
    extended = jnp.concatenate([nodes] + received, axis=0)
    source_hot = one_hot(edge_source, extended.shape[0])
    target_hot = one_hot(edge_target, count_rows)
    source_side = low(product(extended, source_weight))
    target_side = low(product(nodes, target_weight))
    edge_linear = product(source_hot, source_side) + product(target_hot, target_side)
    edge_hidden = low(jax.nn.silu(edge_linear))
    message_linear = product(edge_hidden, edge_weight)
    aggregate = low(left_product(target_hot, low(jax.nn.silu(message_linear))))
    joined = jnp.concatenate([nodes, aggregate], axis=1)
    node_linear = product(joined, inner_weight)
    node_hidden = low(jax.nn.silu(node_linear))
    refined = low(nodes.astype(jnp.float32) + product(node_hidden, outer_weight))
    coarse = low(toward_owners(refined) / count)
    coarse_linear = product(coarse, coarse_weight)
    coarse_update = low(jax.nn.silu(coarse_linear))
    grad_coarse = low(pooled_cotangent * silu_slope(coarse_linear))
    coarse_share = low(right_product(grad_coarse, coarse_weight) / count)
    share_rows = toward_sources(coarse_share)
    updated = low(refined.astype(jnp.float32) + toward_sources(coarse_update))
    coarse_gradient = left_product(coarse, grad_coarse)
    grad_refined = cotangent.astype(jnp.float32) + share_rows
    refined_low = low(grad_refined)
    outer_gradient = left_product(node_hidden, refined_low)
    grad_hidden = low(right_product(refined_low, outer_weight) * silu_slope(node_linear))
    inner_gradient = left_product(joined, grad_hidden)
    grad_joined = right_product(grad_hidden, inner_weight)
    grad_aggregate = low(grad_joined[:, width:])
    grad_message = low(product(target_hot, grad_aggregate) * silu_slope(message_linear))
    edge_gradient = left_product(edge_hidden, grad_message)
    grad_edges = low(right_product(grad_message, edge_weight) * silu_slope(edge_linear))
    grad_sources = low(left_product(source_hot, grad_edges))
    grad_targets = low(left_product(target_hot, grad_edges))
    source_gradient = left_product(extended, grad_sources)
    target_gradient = left_product(nodes, grad_targets)
    gradients = (
        source_gradient,
        target_gradient,
        edge_gradient,
        inner_gradient,
        outer_gradient,
        coarse_gradient,
    )
    sizes = [gradient.shape[0] for gradient in gradients]
    stacked = jnp.concatenate([low(gradient * scale) for gradient in gradients], axis=0)
    summed = summed_over_devices(stacked).astype(jnp.float32)
    starts = [sum(sizes[:number]) for number in range(len(sizes))]
    totals = [
        lax.slice_in_dim(summed, start, start + size, axis=0)
        for start, size in zip(starts, sizes)
    ]
    grad_extended = right_product(grad_sources, source_weight)
    back_blocks = low(grad_extended[count_rows:]).reshape(4, halo_rows, width)
    returned = trade_halo([back_blocks[number] for number in range(4)], -1)
    node_gradient = (
        grad_refined
        + grad_joined[:, :width]
        + right_product(grad_targets, target_weight)
        + grad_extended[:count_rows]
        + left_product(list_hot, jnp.concatenate(returned, axis=0))
    )
    return (updated, node_gradient, *totals)


def solution(mesh):
    in_specs = (
        P(("row", "col"), None),
        P(("row", "col"), None),
        P(("row", "col")),
        P(("row", "col")),
        P(("row", "col"), None, None),
        P(("row", "col")),
        P(("row", "col"), None),
        P(),
        P(),
        P(),
        P(),
        P(),
        P(),
    )
    out_specs = (P(("row", "col"), None), P(("row", "col"), None), P(), P(), P(), P(), P(), P())
    return jax.shard_map(local, mesh=mesh, in_specs=in_specs, out_specs=out_specs, check_vma=False)
```

```python
import functools
import math

import jax
import jax.numpy as jnp
from jax import lax
from jax.experimental import pallas as pl
from jax.experimental.pallas import tpu as pltpu
from jax.sharding import PartitionSpec as P


def passed_along(value, axis, steps):
    count = lax.axis_size(axis)
    initial, last = (max(0, -steps), min(count, count - steps))
    return lax.ppermute(value, axis, [(source, source + steps) for source in range(initial, last)])


def product(first, second):
    return jnp.dot(first, second, preferred_element_type=jnp.float32)


def left_product(first, second):
    return lax.dot_general(
        first, second, (((0,), (0,)), ((), ())), preferred_element_type=jnp.float32
    )


def right_product(first, second):
    return lax.dot_general(
        first, second, (((1,), (1,)), ((), ())), preferred_element_type=jnp.float32
    )


def silu_slope(value):
    sigma = jax.nn.sigmoid(value)
    return sigma * (1.0 + value * (1.0 - sigma))


def one_hot(index, rows):
    return (index[:, None] == jnp.arange(rows, dtype=jnp.int32)[None, :]).astype(jnp.bfloat16)


def low(value):
    return value.astype(jnp.bfloat16)


def trade_halo(blocks, flip):
    moved = []
    for number, offset in enumerate((1, -1)):
        moved.append(passed_along(blocks[number], "row", offset * flip))
    for number, offset in enumerate((1, -1)):
        moved.append(passed_along(blocks[2 + number], "col", offset * flip))
    return moved


def trade_slots(buffer):
    return lax.all_to_all(buffer, ("row", "col"), split_axis=0, concat_axis=0, tiled=True)


class Summation:
    def __init__(self, rows, cols, own, land, out, send, recv):
        self.rows, self.cols, self.devices = rows, cols, rows * cols
        self.bits = cols.bit_length() - 1
        self.own, self.land, self.out, self.send, self.recv = own, land, out, send, recv
        self.row, self.col = lax.axis_index("row"), lax.axis_index("col")
        self.orders = []
        rest = list(range(1, self.bits))
        for half in range(2):
            self.orders.append([0] + (rest if half == 0 else rest[::-1]))
        self.bases = []
        for order in self.orders:
            base, bases = jnp.int32(0), [jnp.int32(0)]
            for stage, bit in enumerate(order):
                base = base + self.digit(bit) * (self.devices >> (stage + 1))
                bases.append(base)
            self.bases.append(bases)
        self.steps = 2 * (self.bits + 1)

    @staticmethod
    def semaphores(rows, cols):
        return 2 * (cols.bit_length() - 1 + rows - 1)

    def digit(self, bit):
        return lax.rem(lax.div(self.col, jnp.int32(1 << bit)), jnp.int32(2))

    def across(self, bit):
        return self.col + (1 - 2 * self.digit(bit)) * (1 << bit)

    def along(self, step):
        return lax.rem(self.row + step, jnp.int32(self.rows))

    def copy(self, half, number, source, target, row, col):
        return pltpu.make_async_remote_copy(
            src_ref=source,
            dst_ref=target,
            send_sem=self.send.at[half, number],
            recv_sem=self.recv.at[half, number],
            device_id=(row, col),
            device_id_type=pl.DeviceIdType.MESH,
        )

    def copies(self, half, step):
        bits, bases = self.bits, self.bases[half]
        found = []
        if step < bits:
            size = self.devices >> (step + 1)
            bit = self.orders[half][step]
            start = bases[step] + (1 - self.digit(bit)) * size
            slot = self.devices - (self.devices >> step)
            found.append(
                self.copy(
                    half,
                    step,
                    self.own.at[half, pl.ds(start, size)],
                    self.land.at[half, pl.ds(slot, size)],
                    self.row,
                    self.across(bit),
                )
            )
        elif step == bits:
            for ahead in range(1, self.rows):
                peer = self.along(ahead)
                found.append(
                    self.copy(
                        half,
                        bits + ahead - 1,
                        self.own.at[half, pl.ds(bases[bits] + peer, 1)],
                        self.land.at[half, pl.ds(self.devices - self.rows + ahead - 1, 1)],
                        peer,
                        self.col,
                    )
                )
        elif step == bits + 1:
            for ahead in range(1, self.rows):
                mine = self.out.at[half, pl.ds(bases[bits] + self.row, 1)]
                found.append(
                    self.copy(
                        half,
                        2 * bits + self.rows - 1 + ahead - 1,
                        mine,
                        mine,
                        self.along(ahead),
                        self.col,
                    )
                )
        else:
            stage = 2 * bits + 1 - step
            size = self.devices >> (stage + 1)
            mine = self.out.at[half, pl.ds(bases[stage + 1], size)]
            found.append(
                self.copy(
                    half,
                    bits + self.rows - 1 + stage,
                    mine,
                    mine,
                    self.row,
                    self.across(self.orders[half][stage]),
                )
            )
        return found

    def start(self, half, step):
        for copy in self.copies(half, step):
            copy.start()

    def finish(self, half, step):
        for copy in self.copies(half, step):
            copy.wait()
        bits, bases = self.bits, self.bases[half]
        if step < bits:
            size = self.devices >> (step + 1)
            slot = self.devices - (self.devices >> step)

            def add(index, carry):
                here = bases[step + 1] + index
                self.own[half, here] = self.own[half, here] + self.land[half, slot + index]
                return carry

            lax.fori_loop(0, size, add, 0)
        elif step == bits:
            total = self.own[half, bases[bits] + self.row].astype(jnp.float32)
            for ahead in range(1, self.rows):
                total += self.land[half, self.devices - self.rows + ahead - 1].astype(jnp.float32)
            self.out[half, bases[bits] + self.row] = total.astype(jnp.bfloat16)

    def begin(self):
        for half in range(2):
            self.start(half, 0)

    def advance(self, step):
        for half in range(2):
            self.finish(half, step)
            if step + 1 < self.steps:
                self.start(half, step + 1)


def hot_rows(column, count):
    spread = lax.broadcasted_iota(jnp.int32, (column.shape[0], count), 1)
    return jnp.where(spread == column, 1.0, 0.0).astype(jnp.bfloat16)


def hot_columns(row, count):
    spread = lax.broadcasted_iota(jnp.int32, (count, row.shape[1]), 0)
    return jnp.where(spread == row, 1.0, 0.0).astype(jnp.bfloat16)


def sigmoid(value):
    return 1.0 / (1.0 + jnp.exp(-value))


def slope(value):
    sigma = sigmoid(value)
    return sigma * (1.0 + value * (1.0 - sigma))


def forward_kernel(
    block,
    nodes,
    halo,
    source_column,
    target_column,
    target_row,
    slot_row,
    source_weight,
    target_weight,
    edge_weight,
    inner_weight,
    outer_weight,
    edge_linear,
    edge_hidden,
    message_linear,
    aggregate,
    node_linear,
    node_hidden,
    refined,
    slots,
    sides,
    sums,
):
    count_rows, width = nodes.shape
    own = nodes[...]
    extra = halo.shape[0]
    sides[0:count_rows, :] = low(product(own, source_weight[...]))
    sides[count_rows : count_rows + extra, :] = low(product(halo[...], source_weight[...]))
    sides[count_rows + extra :, :] = low(product(own, target_weight[...]))
    sums[...] = jnp.zeros_like(sums)

    @pl.loop(0, edge_linear.shape[0] // block)
    def _(number):
        here = pl.ds(pl.multiple_of(number * block, block), block)
        linear = product(
            hot_rows(source_column[here, :], count_rows + extra), sides[0 : count_rows + extra, :]
        )
        linear += product(hot_rows(target_column[here, :], count_rows), sides[count_rows + extra :, :])
        edge_linear[here, :] = low(linear)
        hidden = low(linear * sigmoid(linear))
        edge_hidden[here, :] = hidden
        message = product(hidden, edge_weight[...])
        message_linear[here, :] = low(message)
        sums[...] += product(
            hot_columns(target_row[number], count_rows), low(message * sigmoid(message))
        )

    gathered = low(sums[...])
    aggregate[...] = gathered
    linear = product(own, inner_weight[0:width, :]) + product(gathered, inner_weight[width:, :])
    node_linear[...] = linear
    hidden = low(linear * sigmoid(linear))
    node_hidden[...] = hidden
    result = low(own.astype(jnp.float32) + product(hidden, outer_weight[...]))
    refined[...] = result
    places = slots.shape[0]
    step = count_rows
    for start in range(0, places, step):
        spread = lax.broadcasted_iota(jnp.int32, (step, count_rows), 0) + start
        hot = jnp.where(spread == slot_row[...], 1.0, 0.0).astype(jnp.bfloat16)
        slots[start : start + step, :] = low(product(hot, result))


def pack(flat, own):
    chunk, half_width = own.shape[2:]

    def move(number, carry):
        for half in range(2):
            own[half, number] = flat[
                pl.ds(pl.multiple_of(number * chunk, 16), chunk),
                half * half_width : (half + 1) * half_width,
            ]
        return carry

    lax.fori_loop(0, own.shape[1], move, 0)


def unpack(out, flat):
    chunk, half_width = out.shape[2:]

    def move(number, carry):
        for half in range(2):
            flat[
                pl.ds(pl.multiple_of(number * chunk, 16), chunk),
                half * half_width : (half + 1) * half_width,
            ] = out[half, number]
        return carry

    lax.fori_loop(0, out.shape[1], move, 0)


def backward_kernel(
    rows,
    cols,
    block,
    scale,
    nodes,
    halo,
    cotangent,
    shares,
    slot_column,
    target_column,
    source_row,
    target_row,
    list_row,
    coarse,
    grad_coarse,
    source_weight,
    target_weight,
    edge_weight,
    inner_weight,
    outer_weight,
    edge_linear,
    edge_hidden,
    message_linear,
    aggregate,
    node_linear,
    node_hidden,
    node_gradient,
    early_sums,
    late_sums,
    early_flat,
    late_flat,
    early_own,
    early_land,
    early_out,
    late_own,
    late_land,
    late_out,
    grad_aggregate,
    source_sums,
    target_sums,
    edge_sums,
    blocks,
    landed,
    early_send,
    early_recv,
    late_send,
    late_recv,
    halo_send,
    halo_recv,
):
    early = Summation(rows, cols, early_own, early_land, early_out, early_send, early_recv)
    late = Summation(rows, cols, late_own, late_land, late_out, late_send, late_recv)
    row, col = early.row, early.col
    neighbours = [
        (lax.rem(row + rows - 1, jnp.int32(rows)), col),
        (lax.rem(row + 1, jnp.int32(rows)), col),
        (row, lax.rem(col + cols - 1, jnp.int32(cols))),
        (row, lax.rem(col + 1, jnp.int32(cols))),
    ]
    barrier = pltpu.get_barrier_semaphore()
    peers = [(row, early.across(bit)) for bit in range(early.bits)]
    peers += [(early.along(ahead), col) for ahead in range(1, rows)]
    peers += neighbours[2:]
    for peer in peers:
        pl.semaphore_signal(barrier, inc=1, device_id=peer, device_id_type=pl.DeviceIdType.MESH)

    count_rows, width = nodes.shape
    extra = halo.shape[0]
    each = extra // 4
    own = nodes[...]
    share_rows = product(hot_rows(slot_column[...], shares.shape[0]), shares[...])
    grad_refined = cotangent[...].astype(jnp.float32) + share_rows
    refined_low = low(grad_refined)
    early_flat[0:width, :] = low(scale * left_product(coarse[...], grad_coarse[...]))
    early_flat[width : 2 * width, :] = low(scale * left_product(node_hidden[...], refined_low))
    grad_hidden = low(right_product(refined_low, outer_weight[...]) * slope(node_linear[...]))
    early_flat[2 * width : 3 * width, :] = low(scale * left_product(own, grad_hidden))
    early_flat[3 * width : 4 * width, :] = low(scale * left_product(aggregate[...], grad_hidden))
    pack(early_flat, early_own)
    pl.semaphore_wait(barrier, len(peers))
    early.begin()
    grad_aggregate[...] = low(right_product(grad_hidden, inner_weight[width:, :]))
    node_gradient[...] = grad_refined + right_product(grad_hidden, inner_weight[0:width, :])
    source_sums[...] = jnp.zeros_like(source_sums)
    target_sums[...] = jnp.zeros_like(target_sums)
    edge_sums[...] = jnp.zeros_like(edge_sums)

    for number in range(edge_linear.shape[0] // block):
        here = pl.ds(number * block, block)
        picked = product(hot_rows(target_column[here, :], count_rows), grad_aggregate[...])
        grad_message = low(picked * slope(message_linear[here, :].astype(jnp.float32)))
        edge_sums[...] += left_product(edge_hidden[here, :], grad_message)
        grad_edges = low(
            right_product(grad_message, edge_weight[...])
            * slope(edge_linear[here, :].astype(jnp.float32))
        )
        source_sums[...] += product(hot_columns(source_row[number], count_rows + extra), grad_edges)
        target_sums[...] += product(hot_columns(target_row[number], count_rows), grad_edges)
        if number < early.steps:
            early.advance(number)
    done = min(edge_linear.shape[0] // block, early.steps)

    grad_sources = low(source_sums[...])
    grad_targets = low(target_sums[...])
    blocks[...] = low(right_product(grad_sources[count_rows:], source_weight[...]))
    returns = []
    for number in range(4):
        here = pl.ds(number * each, each)
        returns.append(
            pltpu.make_async_remote_copy(
                src_ref=blocks.at[here],
                dst_ref=landed.at[here],
                send_sem=halo_send.at[number],
                recv_sem=halo_recv.at[number],
                device_id=neighbours[number],
                device_id_type=pl.DeviceIdType.MESH,
            )
        )
    for copy in returns:
        copy.start()
    if late_flat.shape[0] > 3 * width:
        late_flat[3 * width :, :] = jnp.zeros_like(late_flat[3 * width :, :])
    late_flat[0:width, :] = low(
        scale
        * (
            left_product(own, grad_sources[:count_rows])
            + left_product(halo[...], grad_sources[count_rows:])
        )
    )
    late_flat[width : 2 * width, :] = low(scale * left_product(own, grad_targets))
    late_flat[2 * width : 3 * width, :] = low(scale * edge_sums[...])
    pack(late_flat, late_own)
    late.begin()
    node_gradient[...] += right_product(grad_targets, target_weight[...]) + right_product(
        grad_sources[:count_rows], source_weight[...]
    )
    for copy in returns:
        copy.wait()
    inside = [row + 1 < rows, row > 0, col + 1 < cols, col > 0]
    for number in range(4):
        here = pl.ds(number * each, each)
        keep = jnp.where(inside[number], 1.0, 0.0).astype(jnp.bfloat16)
        landed[here, :] = landed[here, :] * keep
    node_gradient[...] += product(hot_columns(list_row[...], count_rows), landed[...])
    for step in range(late.steps):
        if done + step < early.steps:
            early.advance(done + step)
            if done + step == early.steps - 1:
                unpack(early_out, early_sums)
        late.advance(step)
    unpack(late_out, late_sums)


def local(
    nodes,
    cotangent,
    edge_source,
    edge_target,
    halo_lists,
    pool_owner,
    pool_table,
    source_weight,
    target_weight,
    edge_weight,
    inner_weight,
    outer_weight,
    coarse_weight,
):
    devices = lax.axis_size("row") * lax.axis_size("col")
    count_rows, width = nodes.shape
    lists = halo_lists[0]
    halo_rows = lists.shape[1]
    table = pool_table[0]
    capacity = table.shape[0] // devices
    coarse_rows = count_rows // 4
    scale = 1.0 / math.sqrt(count_rows * devices)
    all_lists = lists.reshape(-1)
    owner_hot = one_hot(pool_owner, devices)
    positions = jnp.arange(count_rows, dtype=jnp.int32)
    lower = (positions[:, None] > positions[None, :]).astype(jnp.bfloat16)
    rank = jnp.sum(product(lower, owner_hot) * owner_hot, axis=1).astype(jnp.int32)
    slot = pool_owner * capacity + rank
    slot_hot = one_hot(slot, devices * capacity)
    member = (jnp.arange(coarse_rows, dtype=jnp.int32)[:, None] == table[None, :]).astype(
        jnp.bfloat16
    )
    count = jnp.maximum(jnp.sum(member, axis=1, dtype=jnp.float32), 1.0)[:, None]

    def toward_owners(values):
        return product(member, trade_slots(low(left_product(slot_hot, values))))

    def toward_sources(values):
        return product(slot_hot, trade_slots(low(left_product(member, values))))

    list_hot = one_hot(all_lists, count_rows)
    picked = low(product(list_hot, nodes)).reshape(4, halo_rows, width)
    received = trade_halo([picked[number] for number in range(4)], 1)
    pooled_cotangent = toward_owners(cotangent)
    halo = jnp.concatenate(received, axis=0)
    edges = edge_source.shape[0]
    block = math.gcd(512, edges)
    source_column, target_column = edge_source[:, None], edge_target[:, None]
    source_row = edge_source.reshape(edges // block, 1, block)
    target_row = edge_target.reshape(edges // block, 1, block)
    shaped = jax.ShapeDtypeStruct
    whole = pl.BlockSpec(memory_space=pltpu.VMEM)
    (
        edge_linear,
        edge_hidden,
        message_linear,
        aggregate,
        node_linear,
        node_hidden,
        refined,
        refined_slots,
    ) = pl.pallas_call(
        functools.partial(forward_kernel, block),
        out_shape=(
            shaped((edges, width), jnp.bfloat16),
            shaped((edges, width), jnp.bfloat16),
            shaped((edges, width), jnp.bfloat16),
            shaped((count_rows, width), jnp.bfloat16),
            shaped((count_rows, width), jnp.float32),
            shaped((count_rows, width), jnp.bfloat16),
            shaped((count_rows, width), jnp.bfloat16),
            shaped((devices * capacity, width), jnp.bfloat16),
        ),
        in_specs=[whole] * 11,
        out_specs=[whole] * 8,
        scratch_shapes=[
            pltpu.VMEM((2 * count_rows + 4 * halo_rows, width), jnp.bfloat16),
            pltpu.VMEM((count_rows, width), jnp.float32),
        ],
        compiler_params=pltpu.CompilerParams(vmem_limit_bytes=40 << 20),
        cost_estimate=pl.CostEstimate(
            flops=6 * edges * width * width * 2, bytes_accessed=16 << 20, transcendentals=0
        ),
    )(
        nodes,
        halo,
        source_column,
        target_column,
        target_row,
        slot[None, :],
        source_weight,
        target_weight,
        edge_weight,
        inner_weight,
        outer_weight,
    )
    coarse = low(product(member, trade_slots(refined_slots)) / count)
    coarse_linear = product(coarse, coarse_weight)
    coarse_update = low(jax.nn.silu(coarse_linear))
    grad_coarse = low(pooled_cotangent * silu_slope(coarse_linear))
    coarse_share = low(right_product(grad_coarse, coarse_weight) / count)
    shares = trade_slots(low(left_product(member, coarse_share)))
    rows, cols = lax.axis_size("row"), lax.axis_size("col")
    semaphores = Summation.semaphores(rows, cols)
    heights = (4 * width, 3 * width)
    chunks = [-(-height // (16 * devices)) * 16 for height in heights]
    flats = [(devices * chunk, width) for chunk in chunks]
    cuts = [(2, devices, chunk, width // 2) for chunk in chunks]
    node_gradient, early_sums, late_sums = pl.pallas_call(
        functools.partial(backward_kernel, rows, cols, block, scale),
        out_shape=(
            shaped((count_rows, width), jnp.float32),
            shaped(flats[0], jnp.bfloat16),
            shaped(flats[1], jnp.bfloat16),
        ),
        in_specs=[whole] * 22,
        out_specs=[whole] * 3,
        scratch_shapes=[pltpu.VMEM(flat, jnp.bfloat16) for flat in flats]
        + [pltpu.VMEM(cuts[0], jnp.bfloat16)] * 3
        + [pltpu.VMEM(cuts[1], jnp.bfloat16)] * 3
        + [
            pltpu.VMEM((count_rows, width), jnp.bfloat16),
            pltpu.VMEM((count_rows + 4 * halo_rows, width), jnp.float32),
            pltpu.VMEM((count_rows, width), jnp.float32),
            pltpu.VMEM((width, width), jnp.float32),
            pltpu.VMEM((4 * halo_rows, width), jnp.bfloat16),
            pltpu.VMEM((4 * halo_rows, width), jnp.bfloat16),
        ]
        + [pltpu.SemaphoreType.DMA((2, semaphores))] * 4
        + [pltpu.SemaphoreType.DMA((4,))] * 2,
        compiler_params=pltpu.CompilerParams(
            collective_id=1, has_side_effects=True, vmem_limit_bytes=56 << 20
        ),
        cost_estimate=pl.CostEstimate(
            flops=8 * edges * width * width * 2, bytes_accessed=24 << 20, transcendentals=0
        ),
    )(
        nodes,
        halo,
        cotangent,
        shares.reshape(devices * capacity, width),
        slot[:, None],
        target_column,
        source_row,
        target_row,
        all_lists[None, :],
        coarse,
        grad_coarse,
        source_weight,
        target_weight,
        edge_weight,
        inner_weight,
        outer_weight,
        edge_linear,
        edge_hidden,
        message_linear,
        aggregate,
        node_linear,
        node_hidden,
    )
    updated = low(refined.astype(jnp.float32) + toward_sources(coarse_update))
    early_sums, late_sums = early_sums.astype(jnp.float32), late_sums.astype(jnp.float32)
    return (
        updated,
        node_gradient,
        late_sums[:width],
        late_sums[width : 2 * width],
        late_sums[2 * width : 3 * width],
        early_sums[2 * width : 4 * width],
        early_sums[width : 2 * width],
        early_sums[:width],
    )


def solution(mesh):
    in_specs = (
        P(("row", "col"), None),
        P(("row", "col"), None),
        P(("row", "col")),
        P(("row", "col")),
        P(("row", "col"), None, None),
        P(("row", "col")),
        P(("row", "col"), None),
        P(),
        P(),
        P(),
        P(),
        P(),
        P(),
    )
    out_specs = (P(("row", "col"), None), P(("row", "col"), None), P(), P(), P(), P(), P(), P())
    return jax.shard_map(local, mesh=mesh, in_specs=in_specs, out_specs=out_specs, check_vma=False)
```

```python
import functools
import math

import jax
import jax.numpy as jnp
from jax import lax
from jax.experimental import pallas as pl
from jax.experimental.pallas import tpu as pltpu
from jax.sharding import PartitionSpec as P


def passed_along(value, axis, steps):
    count = lax.axis_size(axis)
    initial, last = (max(0, -steps), min(count, count - steps))
    return lax.ppermute(value, axis, [(source, source + steps) for source in range(initial, last)])


def product(first, second):
    return jnp.dot(first, second, preferred_element_type=jnp.float32)


def left_product(first, second):
    return lax.dot_general(
        first, second, (((0,), (0,)), ((), ())), preferred_element_type=jnp.float32
    )


def right_product(first, second):
    return lax.dot_general(
        first, second, (((1,), (1,)), ((), ())), preferred_element_type=jnp.float32
    )


def silu_slope(value):
    sigma = jax.nn.sigmoid(value)
    return sigma * (1.0 + value * (1.0 - sigma))


def one_hot(index, rows):
    return (index[:, None] == jnp.arange(rows, dtype=jnp.int32)[None, :]).astype(jnp.bfloat16)


def low(value):
    return value.astype(jnp.bfloat16)


def trade_halo(blocks, flip):
    moved = []
    for number, offset in enumerate((1, -1)):
        moved.append(passed_along(blocks[number], "row", offset * flip))
    for number, offset in enumerate((1, -1)):
        moved.append(passed_along(blocks[2 + number], "col", offset * flip))
    return moved


def trade_slots(buffer):
    return lax.all_to_all(buffer, ("row", "col"), split_axis=0, concat_axis=0, tiled=True)


class Summation:
    def __init__(self, rows, cols, own, land, out, send, recv):
        self.rows, self.cols, self.devices = rows, cols, rows * cols
        self.bits = cols.bit_length() - 1
        self.own, self.land, self.out, self.send, self.recv = own, land, out, send, recv
        self.row, self.col = lax.axis_index("row"), lax.axis_index("col")
        self.orders = []
        rest = list(range(1, self.bits))
        for half in range(2):
            self.orders.append([0] + (rest if half == 0 else rest[::-1]))
        self.bases = []
        for order in self.orders:
            base, bases = jnp.int32(0), [jnp.int32(0)]
            for stage, bit in enumerate(order):
                base = base + self.digit(bit) * (self.devices >> (stage + 1))
                bases.append(base)
            self.bases.append(bases)
        self.steps = 2 * (self.bits + 1)

    @staticmethod
    def semaphores(rows, cols):
        return 2 * (cols.bit_length() - 1 + rows - 1)

    def digit(self, bit):
        return lax.rem(lax.div(self.col, jnp.int32(1 << bit)), jnp.int32(2))

    def across(self, bit):
        return self.col + (1 - 2 * self.digit(bit)) * (1 << bit)

    def along(self, step):
        return lax.rem(self.row + step, jnp.int32(self.rows))

    def copy(self, half, number, source, target, row, col):
        return pltpu.make_async_remote_copy(
            src_ref=source,
            dst_ref=target,
            send_sem=self.send.at[half, number],
            recv_sem=self.recv.at[half, number],
            device_id=(row, col),
            device_id_type=pl.DeviceIdType.MESH,
        )

    def copies(self, half, step):
        bits, bases = self.bits, self.bases[half]
        found = []
        if step < bits:
            size = self.devices >> (step + 1)
            bit = self.orders[half][step]
            start = bases[step] + (1 - self.digit(bit)) * size
            slot = self.devices - (self.devices >> step)
            found.append(
                self.copy(
                    half,
                    step,
                    self.own.at[half, pl.ds(start, size)],
                    self.land.at[half, pl.ds(slot, size)],
                    self.row,
                    self.across(bit),
                )
            )
        elif step == bits:
            for ahead in range(1, self.rows):
                peer = self.along(ahead)
                found.append(
                    self.copy(
                        half,
                        bits + ahead - 1,
                        self.own.at[half, pl.ds(bases[bits] + peer, 1)],
                        self.land.at[half, pl.ds(self.devices - self.rows + ahead - 1, 1)],
                        peer,
                        self.col,
                    )
                )
        elif step == bits + 1:
            for ahead in range(1, self.rows):
                mine = self.out.at[half, pl.ds(bases[bits] + self.row, 1)]
                found.append(
                    self.copy(
                        half,
                        2 * bits + self.rows - 1 + ahead - 1,
                        mine,
                        mine,
                        self.along(ahead),
                        self.col,
                    )
                )
        else:
            stage = 2 * bits + 1 - step
            size = self.devices >> (stage + 1)
            mine = self.out.at[half, pl.ds(bases[stage + 1], size)]
            found.append(
                self.copy(
                    half,
                    bits + self.rows - 1 + stage,
                    mine,
                    mine,
                    self.row,
                    self.across(self.orders[half][stage]),
                )
            )
        return found

    def start(self, half, step):
        for copy in self.copies(half, step):
            copy.start()

    def finish(self, half, step):
        for copy in self.copies(half, step):
            copy.wait()
        bits, bases = self.bits, self.bases[half]
        if step < bits:
            size = self.devices >> (step + 1)
            slot = self.devices - (self.devices >> step)

            def add(index, carry):
                here = bases[step + 1] + index
                self.own[half, here] = self.own[half, here] + self.land[half, slot + index]
                return carry

            lax.fori_loop(0, size, add, 0)
        elif step == bits:
            total = self.own[half, bases[bits] + self.row].astype(jnp.float32)
            for ahead in range(1, self.rows):
                total += self.land[half, self.devices - self.rows + ahead - 1].astype(jnp.float32)
            self.out[half, bases[bits] + self.row] = total.astype(jnp.bfloat16)

    def begin(self):
        for half in range(2):
            self.start(half, 0)

    def advance(self, step):
        for half in range(2):
            self.finish(half, step)
            if step + 1 < self.steps:
                self.start(half, step + 1)


def hot_rows(column, count):
    spread = lax.broadcasted_iota(jnp.int32, (column.shape[0], count), 1)
    return jnp.where(spread == column, 1.0, 0.0).astype(jnp.bfloat16)


def hot_columns(row, count):
    spread = lax.broadcasted_iota(jnp.int32, (count, row.shape[1]), 0)
    return jnp.where(spread == row, 1.0, 0.0).astype(jnp.bfloat16)


def sigmoid(value):
    return 1.0 / (1.0 + jnp.exp(-value))


def slope(value):
    sigma = sigmoid(value)
    return sigma * (1.0 + value * (1.0 - sigma))


class Trade:
    def __init__(self, rows, cols, away, home, send, recv):
        self.devices, self.cols = rows * cols, cols
        self.away, self.home, self.send, self.recv = away, home, send, recv
        self.me = lax.axis_index("row") * cols + lax.axis_index("col")

    def place(self, ahead):
        peer = lax.rem(self.me + ahead, jnp.int32(self.devices))
        return peer, (lax.div(peer, jnp.int32(self.cols)), lax.rem(peer, jnp.int32(self.cols)))

    def copy(self, ahead):
        peer, position = self.place(ahead)
        return pltpu.make_async_remote_copy(
            src_ref=self.away.at[peer],
            dst_ref=self.home.at[self.me],
            send_sem=self.send.at[ahead],
            recv_sem=self.recv.at[ahead],
            device_id=position,
            device_id_type=pl.DeviceIdType.MESH,
        )

    def greet(self, barrier):
        def signal(ahead, carry):
            pl.semaphore_signal(
                barrier,
                inc=1,
                device_id=self.place(ahead)[1],
                device_id_type=pl.DeviceIdType.MESH,
            )
            return carry

        lax.fori_loop(1, self.devices, signal, 0)

    def start(self):
        def begin(ahead, carry):
            self.copy(ahead).start()
            return carry

        lax.fori_loop(1, self.devices, begin, 0)
        self.home[self.me] = self.away[self.me]

    def finish(self):
        def end(ahead, carry):
            self.copy(ahead).wait()
            return carry

        lax.fori_loop(1, self.devices, end, 0)

    def rows(self):
        return self.home[...].reshape(self.devices * self.home.shape[1], self.home.shape[2])


def fill_slots(slot_row, values, slots):
    devices, capacity, width = slots.shape
    group = max(1, 512 // capacity)
    for start in range(0, devices, group):
        count = min(group, devices - start)
        spread = lax.broadcasted_iota(jnp.int32, (count * capacity, slot_row.shape[1]), 0)
        hot = jnp.where(spread + start * capacity == slot_row, 1.0, 0.0).astype(jnp.bfloat16)
        slots[start : start + count] = low(product(hot, values)).reshape(count, capacity, width)


def ring_neighbours(rows, cols):
    row, col = lax.axis_index("row"), lax.axis_index("col")
    return [
        (lax.rem(row + rows - 1, jnp.int32(rows)), col),
        (lax.rem(row + 1, jnp.int32(rows)), col),
        (row, lax.rem(col + cols - 1, jnp.int32(cols))),
        (row, lax.rem(col + 1, jnp.int32(cols))),
    ]


def forward_kernel(
    rows,
    cols,
    block,
    nodes,
    cotangent,
    list_column,
    slot_column,
    table_row,
    table_column,
    coarse_weight,
    source_column,
    target_column,
    target_row,
    slot_row,
    source_weight,
    target_weight,
    edge_weight,
    inner_weight,
    outer_weight,
    edge_linear,
    edge_hidden,
    message_linear,
    aggregate,
    node_linear,
    node_hidden,
    refined,
    halo,
    share_rows,
    coarse,
    grad_coarse,
    update_slots,
    sides,
    sums,
    picked,
    landed,
    first_away,
    first_home,
    second_away,
    second_home,
    third_away,
    third_home,
    first_send,
    first_recv,
    second_send,
    second_recv,
    third_send,
    third_recv,
    halo_send,
    halo_recv,
):
    first = Trade(rows, cols, first_away, first_home, first_send, first_recv)
    second = Trade(rows, cols, second_away, second_home, second_send, second_recv)
    third = Trade(rows, cols, third_away, third_home, third_send, third_recv)
    barrier = pltpu.get_barrier_semaphore()
    first.greet(barrier)
    count_rows, width = nodes.shape
    own = nodes[...]
    extra = halo.shape[0]
    each = extra // 4
    picked[...] = low(product(hot_rows(list_column[...], count_rows), own))
    fill_slots(slot_row[...], cotangent[...], first_away)
    pl.semaphore_wait(barrier, rows * cols - 1)
    neighbours = ring_neighbours(rows, cols)
    row, col = lax.axis_index("row"), lax.axis_index("col")
    sends = []
    for number, target in enumerate((1, 0, 3, 2)):
        here = pl.ds(number * each, each)
        sends.append(
            pltpu.make_async_remote_copy(
                src_ref=picked.at[here],
                dst_ref=landed.at[here],
                send_sem=halo_send.at[number],
                recv_sem=halo_recv.at[number],
                device_id=neighbours[target],
                device_id_type=pl.DeviceIdType.MESH,
            )
        )
    for copy in sends:
        copy.start()
    first.start()
    sides[0:count_rows, :] = low(product(own, source_weight[...]))
    sides[count_rows + extra :, :] = low(product(own, target_weight[...]))
    for copy in sends:
        copy.wait()
    inside = [row > 0, row + 1 < rows, col > 0, col + 1 < cols]
    for number in range(4):
        here = pl.ds(number * each, each)
        keep = jnp.where(inside[number], 1.0, 0.0).astype(jnp.bfloat16)
        halo[here, :] = landed[here, :] * keep
    sides[count_rows : count_rows + extra, :] = low(product(halo[...], source_weight[...]))
    sums[...] = jnp.zeros_like(sums)

    @pl.loop(0, edge_linear.shape[0] // block)
    def _(number):
        here = pl.ds(pl.multiple_of(number * block, block), block)
        linear = product(
            hot_rows(source_column[here, :], count_rows + extra), sides[0 : count_rows + extra, :]
        )
        linear += product(hot_rows(target_column[here, :], count_rows), sides[count_rows + extra :, :])
        edge_linear[here, :] = low(linear)
        hidden = low(linear * sigmoid(linear))
        edge_hidden[here, :] = hidden
        message = product(hidden, edge_weight[...])
        message_linear[here, :] = low(message)
        sums[...] += product(
            hot_columns(target_row[number], count_rows), low(message * sigmoid(message))
        )

    gathered = low(sums[...])
    aggregate[...] = gathered
    linear = product(own, inner_weight[0:width, :]) + product(gathered, inner_weight[width:, :])
    node_linear[...] = linear
    hidden = low(linear * sigmoid(linear))
    node_hidden[...] = hidden
    result = low(own.astype(jnp.float32) + product(hidden, outer_weight[...]))
    refined[...] = result
    fill_slots(slot_row[...], result, second_away)
    second.start()
    member = hot_columns(table_row[...], count_rows // 4)
    count = jnp.maximum(jnp.sum(member.astype(jnp.float32), axis=1, keepdims=True), 1.0)
    first.finish()
    pooled_cotangent = product(member, first.rows())
    second.finish()
    pooled = low(product(member, second.rows()) / count)
    coarse[...] = pooled
    linear = product(pooled, coarse_weight[...])
    gradient = low(pooled_cotangent * slope(linear))
    grad_coarse[...] = gradient
    share = low(right_product(gradient, coarse_weight[...]) / count)
    spread = hot_rows(table_column[...], count_rows // 4)
    third_away[...] = low(product(spread, share)).reshape(third_away.shape)
    third.start()
    update = low(linear * sigmoid(linear))
    update_slots[...] = low(product(spread, update)).reshape(update_slots.shape)
    third.finish()
    places = third_home.shape[0] * third_home.shape[1]
    share_rows[...] = product(hot_rows(slot_column[...], places), third.rows())


def pack(flat, own):
    chunk, half_width = own.shape[2:]

    def move(number, carry):
        for half in range(2):
            own[half, number] = flat[
                pl.ds(pl.multiple_of(number * chunk, 16), chunk),
                half * half_width : (half + 1) * half_width,
            ]
        return carry

    lax.fori_loop(0, own.shape[1], move, 0)


def unpack(out, flat):
    chunk, half_width = out.shape[2:]

    def move(number, carry):
        for half in range(2):
            flat[
                pl.ds(pl.multiple_of(number * chunk, 16), chunk),
                half * half_width : (half + 1) * half_width,
            ] = out[half, number]
        return carry

    lax.fori_loop(0, out.shape[1], move, 0)


def backward_kernel(
    rows,
    cols,
    block,
    scale,
    nodes,
    halo,
    cotangent,
    share_rows,
    refined,
    update_slots,
    slot_column,
    target_column,
    source_row,
    target_row,
    list_row,
    coarse,
    grad_coarse,
    source_weight,
    target_weight,
    edge_weight,
    inner_weight,
    outer_weight,
    edge_linear,
    edge_hidden,
    message_linear,
    aggregate,
    node_linear,
    node_hidden,
    node_gradient,
    updated,
    early_sums,
    late_sums,
    early_flat,
    late_flat,
    early_own,
    early_land,
    early_out,
    late_own,
    late_land,
    late_out,
    grad_aggregate,
    source_sums,
    target_sums,
    edge_sums,
    blocks,
    landed,
    update_away,
    update_home,
    update_send,
    update_recv,
    early_send,
    early_recv,
    late_send,
    late_recv,
    halo_send,
    halo_recv,
):
    early = Summation(rows, cols, early_own, early_land, early_out, early_send, early_recv)
    late = Summation(rows, cols, late_own, late_land, late_out, late_send, late_recv)
    row, col = early.row, early.col
    neighbours = ring_neighbours(rows, cols)
    trade = Trade(rows, cols, update_away, update_home, update_send, update_recv)
    barrier = pltpu.get_barrier_semaphore()
    trade.greet(barrier)

    count_rows, width = nodes.shape
    extra = halo.shape[0]
    each = extra // 4
    own = nodes[...]
    grad_refined = cotangent[...].astype(jnp.float32) + share_rows[...]
    refined_low = low(grad_refined)
    early_flat[0:width, :] = low(scale * left_product(coarse[...], grad_coarse[...]))
    early_flat[width : 2 * width, :] = low(scale * left_product(node_hidden[...], refined_low))
    grad_hidden = low(right_product(refined_low, outer_weight[...]) * slope(node_linear[...]))
    early_flat[2 * width : 3 * width, :] = low(scale * left_product(own, grad_hidden))
    early_flat[3 * width : 4 * width, :] = low(scale * left_product(aggregate[...], grad_hidden))
    pack(early_flat, early_own)
    update_away[...] = update_slots[...]
    pl.semaphore_wait(barrier, rows * cols - 1)
    early.begin()
    trade.start()
    grad_aggregate[...] = low(right_product(grad_hidden, inner_weight[width:, :]))
    node_gradient[...] = grad_refined + right_product(grad_hidden, inner_weight[0:width, :])
    source_sums[...] = jnp.zeros_like(source_sums)
    target_sums[...] = jnp.zeros_like(target_sums)
    edge_sums[...] = jnp.zeros_like(edge_sums)

    for number in range(edge_linear.shape[0] // block):
        here = pl.ds(number * block, block)
        picked = product(hot_rows(target_column[here, :], count_rows), grad_aggregate[...])
        grad_message = low(picked * slope(message_linear[here, :].astype(jnp.float32)))
        edge_sums[...] += left_product(edge_hidden[here, :], grad_message)
        grad_edges = low(
            right_product(grad_message, edge_weight[...])
            * slope(edge_linear[here, :].astype(jnp.float32))
        )
        source_sums[...] += product(hot_columns(source_row[number], count_rows + extra), grad_edges)
        target_sums[...] += product(hot_columns(target_row[number], count_rows), grad_edges)
        if number < early.steps:
            early.advance(number)
    done = min(edge_linear.shape[0] // block, early.steps)

    grad_sources = low(source_sums[...])
    grad_targets = low(target_sums[...])
    blocks[...] = low(right_product(grad_sources[count_rows:], source_weight[...]))
    returns = []
    for number in range(4):
        here = pl.ds(number * each, each)
        returns.append(
            pltpu.make_async_remote_copy(
                src_ref=blocks.at[here],
                dst_ref=landed.at[here],
                send_sem=halo_send.at[number],
                recv_sem=halo_recv.at[number],
                device_id=neighbours[number],
                device_id_type=pl.DeviceIdType.MESH,
            )
        )
    for copy in returns:
        copy.start()
    if late_flat.shape[0] > 3 * width:
        late_flat[3 * width :, :] = jnp.zeros_like(late_flat[3 * width :, :])
    late_flat[0:width, :] = low(
        scale
        * (
            left_product(own, grad_sources[:count_rows])
            + left_product(halo[...], grad_sources[count_rows:])
        )
    )
    late_flat[width : 2 * width, :] = low(scale * left_product(own, grad_targets))
    late_flat[2 * width : 3 * width, :] = low(scale * edge_sums[...])
    pack(late_flat, late_own)
    late.begin()
    node_gradient[...] += right_product(grad_targets, target_weight[...]) + right_product(
        grad_sources[:count_rows], source_weight[...]
    )
    for copy in returns:
        copy.wait()
    inside = [row + 1 < rows, row > 0, col + 1 < cols, col > 0]
    for number in range(4):
        here = pl.ds(number * each, each)
        keep = jnp.where(inside[number], 1.0, 0.0).astype(jnp.bfloat16)
        landed[here, :] = landed[here, :] * keep
    node_gradient[...] += product(hot_columns(list_row[...], count_rows), landed[...])
    trade.finish()
    places = update_home.shape[0] * update_home.shape[1]
    updated[...] = low(
        refined[...].astype(jnp.float32) + product(hot_rows(slot_column[...], places), trade.rows())
    )
    for step in range(late.steps):
        if done + step < early.steps:
            early.advance(done + step)
            if done + step == early.steps - 1:
                unpack(early_out, early_sums)
        late.advance(step)
    unpack(late_out, late_sums)


def local(
    nodes,
    cotangent,
    edge_source,
    edge_target,
    halo_lists,
    pool_owner,
    pool_table,
    source_weight,
    target_weight,
    edge_weight,
    inner_weight,
    outer_weight,
    coarse_weight,
):
    devices = lax.axis_size("row") * lax.axis_size("col")
    count_rows, width = nodes.shape
    lists = halo_lists[0]
    halo_rows = lists.shape[1]
    table = pool_table[0]
    capacity = table.shape[0] // devices
    coarse_rows = count_rows // 4
    scale = 1.0 / math.sqrt(count_rows * devices)
    all_lists = lists.reshape(-1)
    room = max(capacity, 16)
    table = jnp.pad(
        table.reshape(devices, capacity), ((0, 0), (0, room - capacity)), constant_values=-1
    ).reshape(devices * room)
    owner_hot = one_hot(pool_owner, devices)
    positions = jnp.arange(count_rows, dtype=jnp.int32)
    lower = (positions[:, None] > positions[None, :]).astype(jnp.bfloat16)
    rank = jnp.sum(product(lower, owner_hot) * owner_hot, axis=1).astype(jnp.int32)
    slot = pool_owner * room + rank
    rows, cols = lax.axis_size("row"), lax.axis_size("col")
    edges = edge_source.shape[0]
    block = math.gcd(512, edges)
    source_column, target_column = edge_source[:, None], edge_target[:, None]
    source_row = edge_source.reshape(edges // block, 1, block)
    target_row = edge_target.reshape(edges // block, 1, block)
    shaped = jax.ShapeDtypeStruct
    whole = pl.BlockSpec(memory_space=pltpu.VMEM)
    (
        edge_linear,
        edge_hidden,
        message_linear,
        aggregate,
        node_linear,
        node_hidden,
        refined,
        halo,
        share_rows,
        coarse,
        grad_coarse,
        update_slots,
    ) = pl.pallas_call(
        functools.partial(forward_kernel, rows, cols, block),
        out_shape=(
            shaped((edges, width), jnp.bfloat16),
            shaped((edges, width), jnp.bfloat16),
            shaped((edges, width), jnp.bfloat16),
            shaped((count_rows, width), jnp.bfloat16),
            shaped((count_rows, width), jnp.float32),
            shaped((count_rows, width), jnp.bfloat16),
            shaped((count_rows, width), jnp.bfloat16),
            shaped((4 * halo_rows, width), jnp.bfloat16),
            shaped((count_rows, width), jnp.float32),
            shaped((coarse_rows, width), jnp.bfloat16),
            shaped((coarse_rows, width), jnp.bfloat16),
            shaped((devices, room, width), jnp.bfloat16),
        ),
        in_specs=[whole] * 16,
        out_specs=[whole] * 12,
        scratch_shapes=[
            pltpu.VMEM((2 * count_rows + 4 * halo_rows, width), jnp.bfloat16),
            pltpu.VMEM((count_rows, width), jnp.float32),
        ]
        + [pltpu.VMEM((4 * halo_rows, width), jnp.bfloat16)] * 2
        + [pltpu.VMEM((devices, room, width), jnp.bfloat16)] * 6
        + [pltpu.SemaphoreType.DMA((devices,))] * 6
        + [pltpu.SemaphoreType.DMA((4,))] * 2,
        compiler_params=pltpu.CompilerParams(
            collective_id=2, has_side_effects=True, vmem_limit_bytes=56 << 20
        ),
        cost_estimate=pl.CostEstimate(
            flops=6 * edges * width * width * 2, bytes_accessed=16 << 20, transcendentals=0
        ),
    )(
        nodes,
        cotangent,
        all_lists[:, None],
        slot[:, None],
        table[None, :],
        table[:, None],
        coarse_weight,
        source_column,
        target_column,
        target_row,
        slot[None, :],
        source_weight,
        target_weight,
        edge_weight,
        inner_weight,
        outer_weight,
    )
    semaphores = Summation.semaphores(rows, cols)
    heights = (4 * width, 3 * width)
    chunks = [-(-height // (16 * devices)) * 16 for height in heights]
    flats = [(devices * chunk, width) for chunk in chunks]
    cuts = [(2, devices, chunk, width // 2) for chunk in chunks]
    node_gradient, updated, early_sums, late_sums = pl.pallas_call(
        functools.partial(backward_kernel, rows, cols, block, scale),
        out_shape=(
            shaped((count_rows, width), jnp.float32),
            shaped((count_rows, width), jnp.bfloat16),
            shaped(flats[0], jnp.bfloat16),
            shaped(flats[1], jnp.bfloat16),
        ),
        in_specs=[whole] * 24,
        out_specs=[whole] * 4,
        scratch_shapes=[pltpu.VMEM(flat, jnp.bfloat16) for flat in flats]
        + [pltpu.VMEM(cuts[0], jnp.bfloat16)] * 3
        + [pltpu.VMEM(cuts[1], jnp.bfloat16)] * 3
        + [
            pltpu.VMEM((count_rows, width), jnp.bfloat16),
            pltpu.VMEM((count_rows + 4 * halo_rows, width), jnp.float32),
            pltpu.VMEM((count_rows, width), jnp.float32),
            pltpu.VMEM((width, width), jnp.float32),
            pltpu.VMEM((4 * halo_rows, width), jnp.bfloat16),
            pltpu.VMEM((4 * halo_rows, width), jnp.bfloat16),
        ]
        + [pltpu.VMEM((devices, room, width), jnp.bfloat16)] * 2
        + [pltpu.SemaphoreType.DMA((devices,))] * 2
        + [pltpu.SemaphoreType.DMA((2, semaphores))] * 4
        + [pltpu.SemaphoreType.DMA((4,))] * 2,
        compiler_params=pltpu.CompilerParams(
            collective_id=1, has_side_effects=True, vmem_limit_bytes=56 << 20
        ),
        cost_estimate=pl.CostEstimate(
            flops=8 * edges * width * width * 2, bytes_accessed=24 << 20, transcendentals=0
        ),
    )(
        nodes,
        halo,
        cotangent,
        share_rows,
        refined,
        update_slots,
        slot[:, None],
        target_column,
        source_row,
        target_row,
        all_lists[None, :],
        coarse,
        grad_coarse,
        source_weight,
        target_weight,
        edge_weight,
        inner_weight,
        outer_weight,
        edge_linear,
        edge_hidden,
        message_linear,
        aggregate,
        node_linear,
        node_hidden,
    )
    early_sums, late_sums = early_sums.astype(jnp.float32), late_sums.astype(jnp.float32)
    return (
        updated,
        node_gradient,
        late_sums[:width],
        late_sums[width : 2 * width],
        late_sums[2 * width : 3 * width],
        early_sums[2 * width : 4 * width],
        early_sums[width : 2 * width],
        early_sums[:width],
    )


def solution(mesh):
    in_specs = (
        P(("row", "col"), None),
        P(("row", "col"), None),
        P(("row", "col")),
        P(("row", "col")),
        P(("row", "col"), None, None),
        P(("row", "col")),
        P(("row", "col"), None),
        P(),
        P(),
        P(),
        P(),
        P(),
        P(),
    )
    out_specs = (P(("row", "col"), None), P(("row", "col"), None), P(), P(), P(), P(), P(), P())
    return jax.shard_map(local, mesh=mesh, in_specs=in_specs, out_specs=out_specs, check_vma=False)
```

```python
import functools
import math

import jax
import jax.numpy as jnp
from jax import lax
from jax.experimental import pallas as pl
from jax.experimental.pallas import tpu as pltpu
from jax.sharding import PartitionSpec as P


def passed_along(value, axis, steps):
    count = lax.axis_size(axis)
    initial, last = (max(0, -steps), min(count, count - steps))
    return lax.ppermute(value, axis, [(source, source + steps) for source in range(initial, last)])


def product(first, second):
    return jnp.dot(first, second, preferred_element_type=jnp.float32)


def left_product(first, second):
    return lax.dot_general(
        first, second, (((0,), (0,)), ((), ())), preferred_element_type=jnp.float32
    )


def right_product(first, second):
    return lax.dot_general(
        first, second, (((1,), (1,)), ((), ())), preferred_element_type=jnp.float32
    )


def silu_slope(value):
    sigma = jax.nn.sigmoid(value)
    return sigma * (1.0 + value * (1.0 - sigma))


def one_hot(index, rows):
    return (index[:, None] == jnp.arange(rows, dtype=jnp.int32)[None, :]).astype(jnp.bfloat16)


def low(value):
    return value.astype(jnp.bfloat16)


def trade_halo(blocks, flip):
    moved = []
    for number, offset in enumerate((1, -1)):
        moved.append(passed_along(blocks[number], "row", offset * flip))
    for number, offset in enumerate((1, -1)):
        moved.append(passed_along(blocks[2 + number], "col", offset * flip))
    return moved


def trade_slots(buffer):
    return lax.all_to_all(buffer, ("row", "col"), split_axis=0, concat_axis=0, tiled=True)


class Summation:
    def __init__(self, rows, cols, own, land, out, send, recv):
        self.rows, self.cols, self.devices = rows, cols, rows * cols
        self.bits = cols.bit_length() - 1
        self.own, self.land, self.out, self.send, self.recv = own, land, out, send, recv
        self.row, self.col = lax.axis_index("row"), lax.axis_index("col")
        self.orders = []
        rest = list(range(1, self.bits))
        for half in range(2):
            self.orders.append([0] + (rest if half == 0 else rest[::-1]))
        self.bases = []
        for order in self.orders:
            base, bases = jnp.int32(0), [jnp.int32(0)]
            for stage, bit in enumerate(order):
                base = base + self.digit(bit) * (self.devices >> (stage + 1))
                bases.append(base)
            self.bases.append(bases)
        self.steps = 2 * (self.bits + 1)

    @staticmethod
    def semaphores(rows, cols):
        return 2 * (cols.bit_length() - 1 + rows - 1)

    def digit(self, bit):
        return lax.rem(lax.div(self.col, jnp.int32(1 << bit)), jnp.int32(2))

    def across(self, bit):
        return self.col + (1 - 2 * self.digit(bit)) * (1 << bit)

    def along(self, step):
        return lax.rem(self.row + step, jnp.int32(self.rows))

    def copy(self, half, number, source, target, row, col):
        return pltpu.make_async_remote_copy(
            src_ref=source,
            dst_ref=target,
            send_sem=self.send.at[half, number],
            recv_sem=self.recv.at[half, number],
            device_id=(row, col),
            device_id_type=pl.DeviceIdType.MESH,
        )

    def copies(self, half, step):
        bits, bases = self.bits, self.bases[half]
        found = []
        if step < bits:
            size = self.devices >> (step + 1)
            bit = self.orders[half][step]
            start = bases[step] + (1 - self.digit(bit)) * size
            slot = self.devices - (self.devices >> step)
            found.append(
                self.copy(
                    half,
                    step,
                    self.own.at[half, pl.ds(start, size)],
                    self.land.at[half, pl.ds(slot, size)],
                    self.row,
                    self.across(bit),
                )
            )
        elif step == bits:
            for ahead in range(1, self.rows):
                peer = self.along(ahead)
                found.append(
                    self.copy(
                        half,
                        bits + ahead - 1,
                        self.own.at[half, pl.ds(bases[bits] + peer, 1)],
                        self.land.at[half, pl.ds(self.devices - self.rows + ahead - 1, 1)],
                        peer,
                        self.col,
                    )
                )
        elif step == bits + 1:
            for ahead in range(1, self.rows):
                mine = self.out.at[half, pl.ds(bases[bits] + self.row, 1)]
                found.append(
                    self.copy(
                        half,
                        2 * bits + self.rows - 1 + ahead - 1,
                        mine,
                        mine,
                        self.along(ahead),
                        self.col,
                    )
                )
        else:
            stage = 2 * bits + 1 - step
            size = self.devices >> (stage + 1)
            mine = self.out.at[half, pl.ds(bases[stage + 1], size)]
            found.append(
                self.copy(
                    half,
                    bits + self.rows - 1 + stage,
                    mine,
                    mine,
                    self.row,
                    self.across(self.orders[half][stage]),
                )
            )
        return found

    def start(self, half, step):
        for copy in self.copies(half, step):
            copy.start()

    def finish(self, half, step):
        for copy in self.copies(half, step):
            copy.wait()
        bits, bases = self.bits, self.bases[half]
        if step < bits:
            size = self.devices >> (step + 1)
            slot = self.devices - (self.devices >> step)

            def add(index, carry):
                here = bases[step + 1] + index
                self.own[half, here] = self.own[half, here] + self.land[half, slot + index]
                return carry

            lax.fori_loop(0, size, add, 0)
        elif step == bits:
            total = self.own[half, bases[bits] + self.row].astype(jnp.float32)
            for ahead in range(1, self.rows):
                total += self.land[half, self.devices - self.rows + ahead - 1].astype(jnp.float32)
            self.out[half, bases[bits] + self.row] = total.astype(jnp.bfloat16)

    def begin(self):
        for half in range(2):
            self.start(half, 0)

    def advance(self, step):
        for half in range(2):
            self.finish(half, step)
            if step + 1 < self.steps:
                self.start(half, step + 1)


def hot_rows(column, count):
    spread = lax.broadcasted_iota(jnp.int32, (column.shape[0], count), 1)
    return jnp.where(spread == column, 1.0, 0.0).astype(jnp.bfloat16)


def hot_columns(row, count):
    spread = lax.broadcasted_iota(jnp.int32, (count, row.shape[1]), 0)
    return jnp.where(spread == row, 1.0, 0.0).astype(jnp.bfloat16)


def sigmoid(value):
    return 1.0 / (1.0 + jnp.exp(-value))


def slope(value):
    sigma = sigmoid(value)
    return sigma * (1.0 + value * (1.0 - sigma))


class Trade:
    def __init__(self, rows, cols, away, home, send, recv):
        self.devices, self.cols = rows * cols, cols
        self.away, self.home, self.send, self.recv = away, home, send, recv
        self.me = lax.axis_index("row") * cols + lax.axis_index("col")

    def place(self, ahead):
        peer = lax.rem(self.me + ahead, jnp.int32(self.devices))
        return peer, (lax.div(peer, jnp.int32(self.cols)), lax.rem(peer, jnp.int32(self.cols)))

    def copy(self, ahead):
        peer, position = self.place(ahead)
        return pltpu.make_async_remote_copy(
            src_ref=self.away.at[peer],
            dst_ref=self.home.at[self.me],
            send_sem=self.send.at[ahead],
            recv_sem=self.recv.at[ahead],
            device_id=position,
            device_id_type=pl.DeviceIdType.MESH,
        )

    def greet(self, barrier):
        def signal(ahead, carry):
            pl.semaphore_signal(
                barrier,
                inc=1,
                device_id=self.place(ahead)[1],
                device_id_type=pl.DeviceIdType.MESH,
            )
            return carry

        lax.fori_loop(1, self.devices, signal, 0)

    def start(self):
        def begin(ahead, carry):
            self.copy(ahead).start()
            return carry

        lax.fori_loop(1, self.devices, begin, 0)
        self.home[self.me] = self.away[self.me]

    def finish(self):
        def end(ahead, carry):
            self.copy(ahead).wait()
            return carry

        lax.fori_loop(1, self.devices, end, 0)

    def rows(self):
        return self.home[...].reshape(self.devices * self.home.shape[1], self.home.shape[2])


def fill_slots(slot_row, values, slots):
    devices, capacity, width = slots.shape
    group = max(1, 512 // capacity)
    for start in range(0, devices, group):
        count = min(group, devices - start)
        spread = lax.broadcasted_iota(jnp.int32, (count * capacity, slot_row.shape[1]), 0)
        hot = jnp.where(spread + start * capacity == slot_row, 1.0, 0.0).astype(jnp.bfloat16)
        slots[start : start + count] = low(product(hot, values)).reshape(count, capacity, width)


def ring_neighbours(rows, cols):
    row, col = lax.axis_index("row"), lax.axis_index("col")
    return [
        (lax.rem(row + rows - 1, jnp.int32(rows)), col),
        (lax.rem(row + 1, jnp.int32(rows)), col),
        (row, lax.rem(col + cols - 1, jnp.int32(cols))),
        (row, lax.rem(col + 1, jnp.int32(cols))),
    ]


def forward_kernel(
    rows,
    cols,
    block,
    nodes,
    cotangent,
    list_column,
    slot_column,
    table_row,
    table_column,
    coarse_weight,
    source_column,
    target_column,
    target_row,
    slot_row,
    source_weight,
    target_weight,
    edge_weight,
    inner_weight,
    outer_weight,
    edge_linear,
    edge_hidden,
    message_linear,
    aggregate,
    node_linear,
    node_hidden,
    refined,
    halo,
    share_rows,
    coarse,
    grad_coarse,
    update_slots,
    sides,
    sums,
    picked,
    landed,
    first_away,
    first_home,
    second_away,
    second_home,
    third_away,
    third_home,
    first_send,
    first_recv,
    second_send,
    second_recv,
    third_send,
    third_recv,
    halo_send,
    halo_recv,
):
    first = Trade(rows, cols, first_away, first_home, first_send, first_recv)
    second = Trade(rows, cols, second_away, second_home, second_send, second_recv)
    third = Trade(rows, cols, third_away, third_home, third_send, third_recv)
    barrier = pltpu.get_barrier_semaphore()
    first.greet(barrier)
    count_rows, width = nodes.shape
    own = nodes[...]
    extra = halo.shape[0]
    each = extra // 4
    picked[...] = low(product(hot_rows(list_column[...], count_rows), own))
    fill_slots(slot_row[...], cotangent[...], first_away)
    pl.semaphore_wait(barrier, rows * cols - 1)
    neighbours = ring_neighbours(rows, cols)
    row, col = lax.axis_index("row"), lax.axis_index("col")
    sends = []
    for number, target in enumerate((1, 0, 3, 2)):
        here = pl.ds(number * each, each)
        sends.append(
            pltpu.make_async_remote_copy(
                src_ref=picked.at[here],
                dst_ref=landed.at[here],
                send_sem=halo_send.at[number],
                recv_sem=halo_recv.at[number],
                device_id=neighbours[target],
                device_id_type=pl.DeviceIdType.MESH,
            )
        )
    for copy in sends:
        copy.start()
    first.start()
    sides[0:count_rows, :] = low(product(own, source_weight[...]))
    sides[count_rows + extra :, :] = low(product(own, target_weight[...]))
    for copy in sends:
        copy.wait()
    inside = [row > 0, row + 1 < rows, col > 0, col + 1 < cols]
    for number in range(4):
        here = pl.ds(number * each, each)
        keep = jnp.where(inside[number], 1.0, 0.0).astype(jnp.bfloat16)
        halo[here, :] = landed[here, :] * keep
    sides[count_rows : count_rows + extra, :] = low(product(halo[...], source_weight[...]))
    sums[...] = jnp.zeros_like(sums)

    @pl.loop(0, edge_linear.shape[0] // block)
    def _(number):
        here = pl.ds(pl.multiple_of(number * block, block), block)
        linear = product(
            hot_rows(source_column[here, :], count_rows + extra), sides[0 : count_rows + extra, :]
        )
        linear += product(hot_rows(target_column[here, :], count_rows), sides[count_rows + extra :, :])
        edge_linear[here, :] = low(linear)
        hidden = low(linear * sigmoid(linear))
        edge_hidden[here, :] = hidden
        message = product(hidden, edge_weight[...])
        message_linear[here, :] = low(message)
        sums[...] += product(
            hot_columns(target_row[number], count_rows), low(message * sigmoid(message))
        )

    gathered = low(sums[...])
    aggregate[...] = gathered
    linear = product(own, inner_weight[0:width, :]) + product(gathered, inner_weight[width:, :])
    node_linear[...] = linear
    hidden = low(linear * sigmoid(linear))
    node_hidden[...] = hidden
    result = low(own.astype(jnp.float32) + product(hidden, outer_weight[...]))
    refined[...] = result
    fill_slots(slot_row[...], result, second_away)
    second.start()
    member = hot_columns(table_row[...], count_rows // 4)
    count = jnp.maximum(jnp.sum(member.astype(jnp.float32), axis=1, keepdims=True), 1.0)
    first.finish()
    pooled_cotangent = product(member, first.rows())
    second.finish()
    pooled = low(product(member, second.rows()) / count)
    coarse[...] = pooled
    linear = product(pooled, coarse_weight[...])
    gradient = low(pooled_cotangent * slope(linear))
    grad_coarse[...] = gradient
    share = low(right_product(gradient, coarse_weight[...]) / count)
    spread = hot_rows(table_column[...], count_rows // 4)
    third_away[...] = low(product(spread, share)).reshape(third_away.shape)
    third.start()
    update = low(linear * sigmoid(linear))
    update_slots[...] = low(product(spread, update)).reshape(update_slots.shape)
    third.finish()
    places = third_home.shape[0] * third_home.shape[1]
    share_rows[...] = product(hot_rows(slot_column[...], places), third.rows())


def pack(flat, own):
    chunk, half_width = own.shape[2:]

    def move(number, carry):
        for half in range(2):
            own[half, number] = flat[
                pl.ds(pl.multiple_of(number * chunk, 16), chunk),
                half * half_width : (half + 1) * half_width,
            ]
        return carry

    lax.fori_loop(0, own.shape[1], move, 0)


def unpack(out, flat):
    chunk, half_width = out.shape[2:]

    def move(number, carry):
        for half in range(2):
            flat[
                pl.ds(pl.multiple_of(number * chunk, 16), chunk),
                half * half_width : (half + 1) * half_width,
            ] = out[half, number]
        return carry

    lax.fori_loop(0, out.shape[1], move, 0)


def backward_kernel(
    rows,
    cols,
    block,
    scale,
    nodes,
    halo,
    cotangent,
    share_rows,
    refined,
    update_slots,
    slot_column,
    target_column,
    source_row,
    target_row,
    list_row,
    coarse,
    grad_coarse,
    source_weight,
    target_weight,
    edge_weight,
    inner_weight,
    outer_weight,
    edge_linear,
    edge_hidden,
    message_linear,
    aggregate,
    node_linear,
    node_hidden,
    node_gradient,
    updated,
    early_sums,
    late_sums,
    early_flat,
    late_flat,
    early_own,
    early_land,
    early_out,
    late_own,
    late_land,
    late_out,
    grad_aggregate,
    source_sums,
    target_sums,
    edge_sums,
    blocks,
    landed,
    update_away,
    update_home,
    update_send,
    update_recv,
    early_send,
    early_recv,
    late_send,
    late_recv,
    halo_send,
    halo_recv,
):
    early = Summation(rows, cols, early_own, early_land, early_out, early_send, early_recv)
    late = Summation(rows, cols, late_own, late_land, late_out, late_send, late_recv)
    row, col = early.row, early.col
    neighbours = ring_neighbours(rows, cols)
    trade = Trade(rows, cols, update_away, update_home, update_send, update_recv)
    barrier = pltpu.get_barrier_semaphore()
    trade.greet(barrier)
    update_away[...] = update_slots[...]
    pl.semaphore_wait(barrier, rows * cols - 1)
    trade.start()

    count_rows, width = nodes.shape
    extra = halo.shape[0]
    each = extra // 4
    own = nodes[...]
    grad_refined = cotangent[...].astype(jnp.float32) + share_rows[...]
    refined_low = low(grad_refined)
    early_flat[0:width, :] = low(scale * left_product(coarse[...], grad_coarse[...]))
    early_flat[width : 2 * width, :] = low(scale * left_product(node_hidden[...], refined_low))
    grad_hidden = low(right_product(refined_low, outer_weight[...]) * slope(node_linear[...]))
    early_flat[2 * width : 3 * width, :] = low(scale * left_product(own, grad_hidden))
    early_flat[3 * width : 4 * width, :] = low(scale * left_product(aggregate[...], grad_hidden))
    pack(early_flat, early_own)
    early.begin()
    grad_aggregate[...] = low(right_product(grad_hidden, inner_weight[width:, :]))
    node_gradient[...] = grad_refined + right_product(grad_hidden, inner_weight[0:width, :])
    source_sums[...] = jnp.zeros_like(source_sums)
    target_sums[...] = jnp.zeros_like(target_sums)
    edge_sums[...] = jnp.zeros_like(edge_sums)

    done = 0
    for number in range(edge_linear.shape[0] // block):
        here = pl.ds(number * block, block)
        picked = product(hot_rows(target_column[here, :], count_rows), grad_aggregate[...])
        grad_message = low(picked * slope(message_linear[here, :].astype(jnp.float32)))
        edge_sums[...] += left_product(edge_hidden[here, :], grad_message)
        grad_edges = low(
            right_product(grad_message, edge_weight[...])
            * slope(edge_linear[here, :].astype(jnp.float32))
        )
        source_sums[...] += product(hot_columns(source_row[number], count_rows + extra), grad_edges)
        target_sums[...] += product(hot_columns(target_row[number], count_rows), grad_edges)
        if number == 1 or number == 3:
            early.advance(done)
            done += 1

    grad_sources = low(source_sums[...])
    grad_targets = low(target_sums[...])
    blocks[...] = low(right_product(grad_sources[count_rows:], source_weight[...]))
    returns = []
    for number in range(4):
        here = pl.ds(number * each, each)
        returns.append(
            pltpu.make_async_remote_copy(
                src_ref=blocks.at[here],
                dst_ref=landed.at[here],
                send_sem=halo_send.at[number],
                recv_sem=halo_recv.at[number],
                device_id=neighbours[number],
                device_id_type=pl.DeviceIdType.MESH,
            )
        )
    for copy in returns:
        copy.start()
    if late_flat.shape[0] > 3 * width:
        late_flat[3 * width :, :] = jnp.zeros_like(late_flat[3 * width :, :])
    late_flat[0:width, :] = low(
        scale
        * (
            left_product(own, grad_sources[:count_rows])
            + left_product(halo[...], grad_sources[count_rows:])
        )
    )
    late_flat[width : 2 * width, :] = low(scale * left_product(own, grad_targets))
    late_flat[2 * width : 3 * width, :] = low(scale * edge_sums[...])
    pack(late_flat, late_own)
    late.begin()
    node_gradient[...] += right_product(grad_targets, target_weight[...]) + right_product(
        grad_sources[:count_rows], source_weight[...]
    )
    for copy in returns:
        copy.wait()
    inside = [row + 1 < rows, row > 0, col + 1 < cols, col > 0]
    for number in range(4):
        here = pl.ds(number * each, each)
        keep = jnp.where(inside[number], 1.0, 0.0).astype(jnp.bfloat16)
        landed[here, :] = landed[here, :] * keep
    node_gradient[...] += product(hot_columns(list_row[...], count_rows), landed[...])
    for step in range(late.steps):
        if done + step < early.steps:
            early.advance(done + step)
            if done + step == early.steps - 1:
                unpack(early_out, early_sums)
        if step == late.steps - 2:
            trade.finish()
            places = update_home.shape[0] * update_home.shape[1]
            updated[...] = low(
                refined[...].astype(jnp.float32)
                + product(hot_rows(slot_column[...], places), trade.rows())
            )
        late.advance(step)
    unpack(late_out, late_sums)


def local(
    nodes,
    cotangent,
    edge_source,
    edge_target,
    halo_lists,
    pool_owner,
    pool_table,
    source_weight,
    target_weight,
    edge_weight,
    inner_weight,
    outer_weight,
    coarse_weight,
):
    devices = lax.axis_size("row") * lax.axis_size("col")
    count_rows, width = nodes.shape
    lists = halo_lists[0]
    halo_rows = lists.shape[1]
    table = pool_table[0]
    capacity = table.shape[0] // devices
    coarse_rows = count_rows // 4
    scale = 1.0 / math.sqrt(count_rows * devices)
    all_lists = lists.reshape(-1)
    room = max(capacity, 16)
    table = jnp.pad(
        table.reshape(devices, capacity), ((0, 0), (0, room - capacity)), constant_values=-1
    ).reshape(devices * room)
    owner_hot = one_hot(pool_owner, devices)
    positions = jnp.arange(count_rows, dtype=jnp.int32)
    lower = (positions[:, None] > positions[None, :]).astype(jnp.bfloat16)
    rank = jnp.sum(product(lower, owner_hot) * owner_hot, axis=1).astype(jnp.int32)
    slot = pool_owner * room + rank
    rows, cols = lax.axis_size("row"), lax.axis_size("col")
    edges = edge_source.shape[0]
    block = math.gcd(512, edges)
    source_column, target_column = edge_source[:, None], edge_target[:, None]
    source_row = edge_source.reshape(edges // block, 1, block)
    target_row = edge_target.reshape(edges // block, 1, block)
    shaped = jax.ShapeDtypeStruct
    whole = pl.BlockSpec(memory_space=pltpu.VMEM)
    (
        edge_linear,
        edge_hidden,
        message_linear,
        aggregate,
        node_linear,
        node_hidden,
        refined,
        halo,
        share_rows,
        coarse,
        grad_coarse,
        update_slots,
    ) = pl.pallas_call(
        functools.partial(forward_kernel, rows, cols, block),
        out_shape=(
            shaped((edges, width), jnp.bfloat16),
            shaped((edges, width), jnp.bfloat16),
            shaped((edges, width), jnp.bfloat16),
            shaped((count_rows, width), jnp.bfloat16),
            shaped((count_rows, width), jnp.float32),
            shaped((count_rows, width), jnp.bfloat16),
            shaped((count_rows, width), jnp.bfloat16),
            shaped((4 * halo_rows, width), jnp.bfloat16),
            shaped((count_rows, width), jnp.float32),
            shaped((coarse_rows, width), jnp.bfloat16),
            shaped((coarse_rows, width), jnp.bfloat16),
            shaped((devices, room, width), jnp.bfloat16),
        ),
        in_specs=[whole] * 16,
        out_specs=[whole] * 12,
        scratch_shapes=[
            pltpu.VMEM((2 * count_rows + 4 * halo_rows, width), jnp.bfloat16),
            pltpu.VMEM((count_rows, width), jnp.float32),
        ]
        + [pltpu.VMEM((4 * halo_rows, width), jnp.bfloat16)] * 2
        + [pltpu.VMEM((devices, room, width), jnp.bfloat16)] * 6
        + [pltpu.SemaphoreType.DMA((devices,))] * 6
        + [pltpu.SemaphoreType.DMA((4,))] * 2,
        compiler_params=pltpu.CompilerParams(
            collective_id=2, has_side_effects=True, vmem_limit_bytes=56 << 20
        ),
        cost_estimate=pl.CostEstimate(
            flops=6 * edges * width * width * 2, bytes_accessed=16 << 20, transcendentals=0
        ),
    )(
        nodes,
        cotangent,
        all_lists[:, None],
        slot[:, None],
        table[None, :],
        table[:, None],
        coarse_weight,
        source_column,
        target_column,
        target_row,
        slot[None, :],
        source_weight,
        target_weight,
        edge_weight,
        inner_weight,
        outer_weight,
    )
    semaphores = Summation.semaphores(rows, cols)
    heights = (4 * width, 3 * width)
    chunks = [-(-height // (16 * devices)) * 16 for height in heights]
    flats = [(devices * chunk, width) for chunk in chunks]
    cuts = [(2, devices, chunk, width // 2) for chunk in chunks]
    node_gradient, updated, early_sums, late_sums = pl.pallas_call(
        functools.partial(backward_kernel, rows, cols, block, scale),
        out_shape=(
            shaped((count_rows, width), jnp.float32),
            shaped((count_rows, width), jnp.bfloat16),
            shaped(flats[0], jnp.bfloat16),
            shaped(flats[1], jnp.bfloat16),
        ),
        in_specs=[whole] * 24,
        out_specs=[whole] * 4,
        scratch_shapes=[pltpu.VMEM(flat, jnp.bfloat16) for flat in flats]
        + [pltpu.VMEM(cuts[0], jnp.bfloat16)] * 3
        + [pltpu.VMEM(cuts[1], jnp.bfloat16)] * 3
        + [
            pltpu.VMEM((count_rows, width), jnp.bfloat16),
            pltpu.VMEM((count_rows + 4 * halo_rows, width), jnp.float32),
            pltpu.VMEM((count_rows, width), jnp.float32),
            pltpu.VMEM((width, width), jnp.float32),
            pltpu.VMEM((4 * halo_rows, width), jnp.bfloat16),
            pltpu.VMEM((4 * halo_rows, width), jnp.bfloat16),
        ]
        + [pltpu.VMEM((devices, room, width), jnp.bfloat16)] * 2
        + [pltpu.SemaphoreType.DMA((devices,))] * 2
        + [pltpu.SemaphoreType.DMA((2, semaphores))] * 4
        + [pltpu.SemaphoreType.DMA((4,))] * 2,
        compiler_params=pltpu.CompilerParams(
            collective_id=1, has_side_effects=True, vmem_limit_bytes=56 << 20
        ),
        cost_estimate=pl.CostEstimate(
            flops=8 * edges * width * width * 2, bytes_accessed=24 << 20, transcendentals=0
        ),
    )(
        nodes,
        halo,
        cotangent,
        share_rows,
        refined,
        update_slots,
        slot[:, None],
        target_column,
        source_row,
        target_row,
        all_lists[None, :],
        coarse,
        grad_coarse,
        source_weight,
        target_weight,
        edge_weight,
        inner_weight,
        outer_weight,
        edge_linear,
        edge_hidden,
        message_linear,
        aggregate,
        node_linear,
        node_hidden,
    )
    early_sums, late_sums = early_sums.astype(jnp.float32), late_sums.astype(jnp.float32)
    return (
        updated,
        node_gradient,
        late_sums[:width],
        late_sums[width : 2 * width],
        late_sums[2 * width : 3 * width],
        early_sums[2 * width : 4 * width],
        early_sums[width : 2 * width],
        early_sums[:width],
    )


def solution(mesh):
    in_specs = (
        P(("row", "col"), None),
        P(("row", "col"), None),
        P(("row", "col")),
        P(("row", "col")),
        P(("row", "col"), None, None),
        P(("row", "col")),
        P(("row", "col"), None),
        P(),
        P(),
        P(),
        P(),
        P(),
        P(),
    )
    out_specs = (P(("row", "col"), None), P(("row", "col"), None), P(), P(), P(), P(), P(), P())
    return jax.shard_map(local, mesh=mesh, in_specs=in_specs, out_specs=out_specs, check_vma=False)
```
